32 devices in a mesh: req: 8 (over z, x), mlp: 4 (over y, core).
Axes of the slice: x: 2, y: 2, z: 4, core: 2. Of those that a mesh axis runs over, the one named last changes fastest.
Arguments:
- drafts: bfloat16 [64, 16, 2048], P('req', None, 'mlp'), may hold values from -60 to 60
- slot_of: int32 [64], replicated, may hold values from 0 to 63, as said below
- lengths: int32 [64], P('req'), may hold values from 2 to 256, as said below
- parents: int32 [64, 16], P('req'), may hold values from 0 to 14, as said below
- accepted_tokens: int32 [64, 8], P('req'), may hold values from 0 to 15, as said below
- cached_key_value: bfloat16 [64, 256, 4, 128], P('req', None, 'mlp'), may hold values from -2000 to 2000
- attn_gain: float32 [2048], replicated, may hold values from 0.1 to 1.9
- query_weight: bfloat16 [2048, 768], P(None, 'mlp'), may hold values from -0.125 to 0.125
- key_value_weight: bfloat16 [2048, 512], P(None, 'mlp'), may hold values from -0.125 to 0.125
- w_out: bfloat16 [768, 2048], P('mlp'), may hold values from -0.21875 to 0.21875
- mlp_gain: float32 [2048], replicated, may hold values from 0.1 to 1.9
- w_gate: bfloat16 [2048, 2560], P(None, 'mlp'), may hold values from -0.125 to 0.125
- w_up: bfloat16 [2048, 2560], P(None, 'mlp'), may hold values from -0.125 to 0.125
- w_down: bfloat16 [2560, 2048], P('mlp'), may hold values from -0.125 to 0.125
Outputs:
- layer_output: bfloat16 [64, 16, 2048], P('req', None, 'mlp')
- accepted_kv: bfloat16 [64, 8, 4, 128], P('req', None, 'mlp')
The draws below stay inside these ranges and needn't reach their ends.
Inputs may be any that keep to these rules, and one draw needn't show every extreme that they name: `slot_of`: A permutation of the 64 slots; the cache of slot s is held by index s // 8 of req. Of the 8 requests that arrive on one index of req, at most 1 have their caches on any one index, and that many do for some. `lengths`: some slot holds exactly 256 cached positions. parents[s, 0] = 0 and parents[s, j] < j for j >= 1. accepted_tokens[s, 0] = 0, the entries rise, and each entry is the parent of the next.
All inputs are finite; a program needn't handle non-finite values.
Results may differ from the reference program's by a relative error of at most 0.0095.
Values may be sent and summed in bfloat16 or wider, within the bound.
A program may use at most 64 MiB of HBM per device.

```python
import math
import jax
import jax.numpy as jnp
from jax import lax

MODEL_DIM = 2048
QUERY_HEADS = 12
KEY_VALUE_HEADS = 4
HEAD_DIM = 64
FFW = 2560
TREE_TOKENS = 16
ACCEPT_LENGTH = 8
CACHE_LIMIT = 256
REQUESTS_PER_KEY = 8
REQUEST_TOTAL = 64
N_REQ = 8
N_MLP = 4


def draw_slot_of(key, part):
    folded = jax.random.fold_in(key, 11)
    key_order, key_shift, key_label, key_local = jax.random.split(folded, 4)
    shift_order = jax.vmap(lambda subkey: jax.random.permutation(subkey, REQUESTS_PER_KEY))(jax.random.split(key_order, N_REQ))
    shifts = jax.random.permutation(key_shift, N_REQ)
    relabel = jax.random.permutation(key_label, N_REQ)
    local_order = jax.vmap(lambda subkey: jax.random.permutation(subkey, REQUESTS_PER_KEY))(jax.random.split(key_local, N_REQ))
    sources = jnp.arange(N_REQ, dtype=jnp.int32)[:, None]
    raw_owner = (sources + shifts[shift_order % N_REQ]) % N_REQ
    owners = relabel[raw_owner]
    local_slot = local_order[owners, shift_order]
    return (owners * REQUESTS_PER_KEY + local_slot).reshape(REQUEST_TOTAL).astype(jnp.int32)


def draw_lengths(key, part):
    key_level, key_len, key_pick = jax.random.split(jax.random.fold_in(key, 23), 3)
    levels = jax.random.randint(key_level, (REQUEST_TOTAL,), 0, 5)
    ceiling = jnp.maximum(CACHE_LIMIT // jnp.left_shift(jnp.int32(1), levels), 2)
    drawn_len = jax.random.randint(key_len, (REQUEST_TOTAL,), 2, ceiling + 1)
    chosen = jax.random.randint(key_pick, (), 0, REQUEST_TOTAL)
    return jnp.where(jnp.arange(REQUEST_TOTAL) == chosen, CACHE_LIMIT, drawn_len).astype(jnp.int32)


def draw_tree(key):
    key_path, key_parent = jax.random.split(jax.random.fold_in(key, 37))
    shuffled = jax.vmap(lambda subkey: jax.random.permutation(subkey, TREE_TOKENS - 1))(jax.random.split(key_path, REQUEST_TOTAL)) + 1
    chosen = jnp.sort(shuffled[:, :ACCEPT_LENGTH - 1], axis=1).astype(jnp.int32)
    tail_path = jnp.arange(TREE_TOKENS - ACCEPT_LENGTH + 1, TREE_TOKENS, dtype=jnp.int32)
    chosen = chosen.at[0].set(tail_path)
    accepted_tokens = jnp.concatenate([jnp.zeros((REQUEST_TOTAL, 1), jnp.int32), chosen], axis=1)
    upper_bound = jnp.maximum(jnp.arange(TREE_TOKENS, dtype=jnp.int32), 1)
    parents = jax.random.randint(key_parent, (REQUEST_TOTAL, TREE_TOKENS), 0, upper_bound[None, :]).astype(jnp.int32)
    row_ids = jnp.arange(REQUEST_TOTAL)[:, None]
    parents = parents.at[row_ids, accepted_tokens[:, 1:]].set(accepted_tokens[:, :-1])
    return (parents.astype(jnp.int32), accepted_tokens.astype(jnp.int32))


def draw_parents(key, part):
    return draw_tree(key)[0]


def draw_accepted_tokens(key, part):
    return draw_tree(key)[1]


def draw_cached_key_value(key, part):
    key_base = jax.random.fold_in(jax.random.fold_in(key, 41), 0)
    complete_shape = (REQUEST_TOTAL, CACHE_LIMIT, KEY_VALUE_HEADS, 2 * HEAD_DIM)
    filled = jax.random.truncated_normal(key_base, -5.0, 5.0, complete_shape, jnp.float32)
    return filled.astype(jnp.bfloat16)


def draw_drafts(key, part):
    key_noise, key_col, key_row = jax.random.split(jax.random.fold_in(key, 53), 3)
    column_log = math.log(3.0) * (jnp.arange(MODEL_DIM, dtype=jnp.float32) / MODEL_DIM - 0.5) + jax.random.uniform(key_col, (MODEL_DIM,), jnp.float32, -0.6, 0.6)
    row_log = jax.random.uniform(key_row, (REQUEST_TOTAL, TREE_TOKENS, 1), jnp.float32, -1.15, 1.15)
    noise = jax.random.truncated_normal(key_noise, -5.0, 5.0, (REQUEST_TOTAL, TREE_TOKENS, MODEL_DIM), jnp.float32)
    return (noise * jnp.exp(column_log + row_log)).astype(jnp.bfloat16)


def shard_levels(own_key, shape, shards, smallest, largest):
    factor_of, own = 1.0, jax.random.fold_in(own_key, 6)
    for position, blocks in shards:
        draws = jnp.exp(jax.random.uniform(jax.random.fold_in(own, position), (blocks,), jnp.float32, smallest / len(shards), largest / len(shards)))
        factor_of = factor_of * jnp.repeat(draws, shape[position] // blocks).reshape([-1 if axis == position else 1 for axis in range(len(shape))])
    return factor_of


def centred(key, shape, spread, limit, cuts=(), kind=jnp.bfloat16):
    loudness = shard_levels(key, shape, cuts, -0.22, 0.18) if cuts else 1.0
    values = jax.random.normal(key, shape, jnp.float32) * spread * loudness
    return jnp.minimum(jnp.maximum(values, -limit), limit).astype(kind)


def setup_inputs(seed: int = 0) -> dict:
    streams_of = jax.random.split(jax.random.key(seed), 15)
    drafts = draw_drafts(jax.random.fold_in(streams_of[14], 71), 0)
    slot_of = draw_slot_of(jax.random.fold_in(streams_of[14], 71), 0)
    lengths = draw_lengths(jax.random.fold_in(streams_of[14], 71), 0)
    parents = draw_parents(jax.random.fold_in(streams_of[14], 71), 0)
    accepted_tokens = draw_accepted_tokens(jax.random.fold_in(streams_of[14], 71), 0)
    cached_key_value = draw_cached_key_value(jax.random.fold_in(streams_of[14], 71), 0)
    attn_gain = jnp.clip(1.0 + 0.18 * jax.random.normal(streams_of[6], (MODEL_DIM,), jnp.float32), 0.1, 1.9)
    query_weight = centred(streams_of[7], (MODEL_DIM, QUERY_HEADS * HEAD_DIM), MODEL_DIM ** -0.5, 0.125, ((1, 4),))
    key_value_weight = centred(streams_of[8], (MODEL_DIM, 2 * KEY_VALUE_HEADS * HEAD_DIM), MODEL_DIM ** -0.5, 0.125, ((1, 4),))
    w_out = centred(streams_of[9], (QUERY_HEADS * HEAD_DIM, MODEL_DIM), (QUERY_HEADS * HEAD_DIM) ** -0.5, 0.21875, ((0, 4),))
    mlp_gain = jnp.clip(1.0 + 0.18 * jax.random.normal(streams_of[10], (MODEL_DIM,), jnp.float32), 0.1, 1.9)
    w_gate = centred(streams_of[11], (MODEL_DIM, FFW), MODEL_DIM ** -0.5, 0.125, ((1, 4),))
    w_up = centred(streams_of[12], (MODEL_DIM, FFW), MODEL_DIM ** -0.5, 0.125, ((1, 4),))
    w_down = centred(streams_of[13], (FFW, MODEL_DIM), FFW ** -0.5, 0.125, ((0, 4),))
    return dict(drafts=drafts, slot_of=slot_of, lengths=lengths, parents=parents, accepted_tokens=accepted_tokens, cached_key_value=cached_key_value, attn_gain=attn_gain, query_weight=query_weight, key_value_weight=key_value_weight, w_out=w_out, mlp_gain=mlp_gain, w_gate=w_gate, w_up=w_up, w_down=w_down)


EPS = 1e-06
HIGH = lax.Precision.HIGHEST

def ancestry(tree_links, tokens):
    parent_link = (tree_links[:, :, None] == jnp.arange(tokens, dtype=jnp.int32)[None, None, :]).astype(jnp.float32)
    reachable = jnp.maximum(parent_link, jnp.eye(tokens, dtype=jnp.float32)[None])
    for squaring in range(max(tokens - 1, 1).bit_length()):
        reachable = jnp.minimum(jnp.einsum('rij,rjk->rik', reachable, reachable, precision=HIGH), 1.0)
    return reachable > 0.5

def rounded(values):
    return lax.optimization_barrier(values.astype(jnp.bfloat16)).astype(jnp.float32)

def rms_norm(matrix_rows, norm_gain):
    return matrix_rows * lax.rsqrt(lax.optimization_barrier(jnp.mean(matrix_rows * matrix_rows, axis=-1, keepdims=True)) + EPS) * norm_gain

def reference(drafts, slot_of, lengths, parents, accepted_tokens, cached_key_value, attn_gain, query_weight, key_value_weight, w_out, mlp_gain, w_gate, w_up, w_down):
    sorted_rows = jnp.zeros_like(drafts).at[slot_of].set(drafts)
    score_scale = 1.0 / math.sqrt(HEAD_DIM)
    head_span = QUERY_HEADS * HEAD_DIM // N_MLP
    unit_span = FFW // N_MLP

    def one_owner(packed):
        owner_rows, cache_len, tree_links, chosen, cache_rows = packed
        per_owner_rows = owner_rows.shape[0]
        flat_rows = owner_rows.reshape(per_owner_rows * TREE_TOKENS, MODEL_DIM).astype(jnp.float32)
        normalized_rows = rms_norm(flat_rows, attn_gain).astype(jnp.bfloat16)
        query_rows = jnp.dot(normalized_rows, query_weight, preferred_element_type=jnp.float32).reshape(per_owner_rows, TREE_TOKENS, KEY_VALUE_HEADS, QUERY_HEADS // KEY_VALUE_HEADS, HEAD_DIM)
        new_key_value = jnp.dot(normalized_rows, key_value_weight, preferred_element_type=jnp.float32).astype(jnp.bfloat16).reshape(per_owner_rows, TREE_TOKENS, KEY_VALUE_HEADS, 2 * HEAD_DIM)
        cache_wide = cache_rows.astype(jnp.float32)
        fresh_wide = new_key_value.astype(jnp.float32)
        score_cache = jnp.einsum('rtkgd,rckd->rkgtc', query_rows, cache_wide[..., :HEAD_DIM], precision=HIGH) * score_scale
        live_rows = jnp.arange(CACHE_LIMIT)[None, :] < cache_len[:, None]
        score_cache = jnp.where(live_rows[:, None, None, None, :], score_cache, -jnp.inf)
        score_draft = jnp.einsum('rtkgd,rjkd->rkgtj', query_rows, fresh_wide[..., :HEAD_DIM], precision=HIGH) * score_scale
        score_draft = jnp.where(ancestry(tree_links, TREE_TOKENS)[:, None, None], score_draft, -jnp.inf)
        row_top = jnp.maximum(lax.optimization_barrier(jnp.max(score_cache, axis=-1)), lax.optimization_barrier(jnp.max(score_draft, axis=-1)))
        weight_cache = rounded(jnp.exp(score_cache - row_top[..., None]))
        weight_draft = rounded(jnp.exp(score_draft - row_top[..., None]))
        numerator = jnp.einsum('rkgtc,rckd->rtkgd', weight_cache, cache_wide[..., HEAD_DIM:], precision=HIGH)
        numerator = numerator + jnp.einsum('rkgtj,rjkd->rtkgd', weight_draft, fresh_wide[..., HEAD_DIM:], precision=HIGH)
        denominator = lax.optimization_barrier(jnp.sum(weight_cache, axis=-1)) + lax.optimization_barrier(jnp.sum(weight_draft, axis=-1))
        attended = (numerator / jnp.transpose(denominator, (0, 3, 1, 2))[..., None]).astype(jnp.bfloat16)
        attended = attended.reshape(per_owner_rows * TREE_TOKENS, QUERY_HEADS * HEAD_DIM)
        attn_sum = jnp.zeros((per_owner_rows * TREE_TOKENS, MODEL_DIM), jnp.float32)
        for group_index in range(N_MLP):
            lower = group_index * head_span
            attn_sum = attn_sum + rounded(jnp.dot(attended[:, lower:lower + head_span], w_out[lower:lower + head_span], preferred_element_type=jnp.float32))
        residual = flat_rows + attn_sum
        normed_two = rms_norm(residual, mlp_gain).astype(jnp.bfloat16)
        gate_out = jnp.dot(normed_two, w_gate, preferred_element_type=jnp.float32)
        up_out = jnp.dot(normed_two, w_up, preferred_element_type=jnp.float32)
        hidden = (jax.nn.silu(gate_out) * up_out).astype(jnp.bfloat16)
        unit_total = jnp.zeros((per_owner_rows * TREE_TOKENS, MODEL_DIM), jnp.float32)
        for group_index in range(N_MLP):
            lower = group_index * unit_span
            unit_total = unit_total + rounded(jnp.dot(hidden[:, lower:lower + unit_span], w_down[lower:lower + unit_span], preferred_element_type=jnp.float32))
        out_rows = (residual + unit_total).astype(jnp.bfloat16).reshape(per_owner_rows, TREE_TOKENS, MODEL_DIM)
        picker = (chosen[:, :, None] == jnp.arange(TREE_TOKENS, dtype=jnp.int32)[None, None, :]).astype(jnp.float32)
        accepted_rows = jnp.einsum('rat,rtkd->rakd', picker, fresh_wide, precision=HIGH).astype(jnp.bfloat16)
        return (out_rows, accepted_rows)
    packed_everything = (sorted_rows.reshape(N_REQ, REQUESTS_PER_KEY, TREE_TOKENS, MODEL_DIM), lengths.reshape(N_REQ, REQUESTS_PER_KEY), parents.reshape(N_REQ, REQUESTS_PER_KEY, TREE_TOKENS), accepted_tokens.reshape(N_REQ, REQUESTS_PER_KEY, ACCEPT_LENGTH), cached_key_value.reshape(N_REQ, REQUESTS_PER_KEY, CACHE_LIMIT, KEY_VALUE_HEADS, 2 * HEAD_DIM))
    out_rows, accepted_rows = lax.map(one_owner, packed_everything)
    owner_out = out_rows.reshape(REQUEST_TOTAL, TREE_TOKENS, MODEL_DIM)
    layer_output = owner_out[slot_of]
    return (layer_output, accepted_rows.reshape(REQUEST_TOTAL, ACCEPT_LENGTH, KEY_VALUE_HEADS, 2 * HEAD_DIM))
```

```python
import math

import jax
import jax.numpy as jnp
from jax import lax
from jax.experimental import pallas as pl
from jax.experimental.pallas import tpu as pltpu
from jax.sharding import PartitionSpec as P

HEAD_DIM = 64


EPS = 1e-06
HIGH = lax.Precision.HIGHEST


def route_tables(slot_of, per_owner_rows, sources, groups, my_index):
    owners = slot_of // per_owner_rows
    owner_grid = owners.reshape(sources, per_owner_rows)
    request_ids = jnp.arange(per_owner_rows)
    earlier = request_ids[None, :] < request_ids[:, None]
    position = jnp.sum((owner_grid[:, :, None] == owner_grid[:, None, :]) & earlier[None], axis=2)
    column = (jnp.arange(sources, dtype=jnp.int32)[:, None] * groups + position).reshape(-1)
    slot_count = sources * groups
    my_owners = lax.dynamic_index_in_dim(owner_grid, my_index, 0, keepdims=False)
    my_position = lax.dynamic_index_in_dim(position, my_index, 0, keepdims=False)
    target = my_owners * groups + my_position
    sender = (jnp.arange(slot_count)[:, None] == target[None, :]).astype(jnp.bfloat16)
    arrive = (slot_of[None, :] == my_index * per_owner_rows + request_ids[:, None]).astype(
        jnp.bfloat16
    )
    places = (column[:, None] == jnp.arange(slot_count)[None, :]).astype(jnp.bfloat16)
    receiver = jnp.dot(arrive, places, preferred_element_type=jnp.float32).astype(jnp.bfloat16)
    return (sender, receiver)


def ancestry(tree_links, tokens):
    parent_link = (
        tree_links[:, :, None] == jnp.arange(tokens, dtype=jnp.int32)[None, None, :]
    ).astype(jnp.float32)
    reachable = jnp.maximum(parent_link, jnp.eye(tokens, dtype=jnp.float32)[None])
    for squaring in range(max(tokens - 1, 1).bit_length()):
        reachable = jnp.minimum(
            jnp.einsum("rij,rjk->rik", reachable, reachable, precision=HIGH), 1.0
        )
    return reachable > 0.5


def cache_scores(query_rows, cache_block, cache_len, score_scale, head_size):
    key_rows = cache_block[..., :head_size].astype(jnp.float32)
    scores = jnp.einsum("rtkgd,rckd->rkgtc", query_rows, key_rows, precision=HIGH) * score_scale
    row_ids = jnp.arange(cache_block.shape[1])
    live_rows = row_ids[None, :] < cache_len[:, None]
    return jnp.where(live_rows[:, None, None, None, :], scores, -jnp.inf)


def weighted(weights, cache_block, head_size):
    return jnp.einsum(
        "rkgtc,rckd->rtkgd",
        weights,
        cache_block[..., head_size:],
        preferred_element_type=jnp.float32,
    )


def per_device(
    drafts,
    slot_of,
    lengths,
    parents,
    accepted_tokens,
    cached_key_value,
    attn_gain,
    query_weight,
    key_value_weight,
    w_out,
    mlp_gain,
    w_gate,
    w_up,
    w_down,
):
    req_count = lax.axis_size("req")
    my_index = lax.axis_index("req")
    part_index = lax.axis_index("mlp")
    per_owner_rows, tokens, quarter = drafts.shape
    sends = max(1, per_owner_rows // req_count)
    sender, receiver = route_tables(slot_of, per_owner_rows, req_count, sends, my_index)
    flat_rows = drafts.reshape(per_owner_rows, tokens * quarter)
    outgoing = jnp.dot(sender, flat_rows, preferred_element_type=jnp.float32).astype(jnp.bfloat16)
    outgoing = outgoing.reshape(req_count, sends, tokens * quarter)
    incoming = lax.all_to_all(outgoing, "req", split_axis=0, concat_axis=0, tiled=True)
    local_rows = jnp.dot(
        receiver,
        incoming.reshape(req_count * sends, tokens * quarter),
        preferred_element_type=jnp.float32,
    ).astype(jnp.bfloat16)
    local_rows = local_rows.reshape(per_owner_rows * tokens, quarter)
    full_rows = lax.all_gather(local_rows, "mlp", axis=1, tiled=True)
    wide_rows = full_rows.astype(jnp.float32)
    normalized_rows = (
        wide_rows
        * lax.rsqrt(jnp.mean(wide_rows * wide_rows, axis=1, keepdims=True) + EPS)
        * attn_gain
    ).astype(jnp.bfloat16)
    kv_heads = key_value_weight.shape[1] // (2 * HEAD_DIM)
    group_heads = query_weight.shape[1] // (kv_heads * HEAD_DIM)
    query_rows = jnp.dot(normalized_rows, query_weight, preferred_element_type=jnp.float32).reshape(
        per_owner_rows, tokens, kv_heads, group_heads, HEAD_DIM
    )
    new_key_value = (
        jnp.dot(normalized_rows, key_value_weight, preferred_element_type=jnp.float32)
        .astype(jnp.bfloat16)
        .reshape(per_owner_rows, tokens, kv_heads, 2 * HEAD_DIM)
    )
    picker = (
        accepted_tokens[:, :, None] == jnp.arange(tokens, dtype=jnp.int32)[None, None, :]
    ).astype(jnp.bfloat16)
    accepted_rows = jnp.einsum(
        "rat,rtkd->rakd", picker, new_key_value, preferred_element_type=jnp.float32
    ).astype(jnp.bfloat16)
    score_scale = 1.0 / math.sqrt(HEAD_DIM)
    draft_keys = new_key_value[..., :HEAD_DIM].astype(jnp.float32)
    draft_scores = (
        jnp.einsum("rtkgd,rjkd->rkgtj", query_rows, draft_keys, precision=HIGH) * score_scale
    )
    draft_scores = jnp.where(ancestry(parents, tokens)[:, None, None], draft_scores, -jnp.inf)
    draft_top = jnp.max(draft_scores, axis=-1)
    scores = cache_scores(query_rows, cached_key_value, lengths, score_scale, HEAD_DIM)
    row_top = jnp.maximum(draft_top, jnp.max(scores, axis=-1))
    weights = jnp.exp(scores - row_top[..., None]).astype(jnp.bfloat16)
    numerator = weighted(weights, cached_key_value, HEAD_DIM)
    denominator = jnp.sum(weights.astype(jnp.float32), axis=-1)
    draft_weights = jnp.exp(draft_scores - row_top[..., None]).astype(jnp.bfloat16)
    numerator = numerator + jnp.einsum(
        "rkgtj,rjkd->rtkgd",
        draft_weights,
        new_key_value[..., HEAD_DIM:],
        preferred_element_type=jnp.float32,
    )
    denominator = denominator + jnp.sum(draft_weights.astype(jnp.float32), axis=-1)
    attended = (numerator / jnp.transpose(denominator, (0, 3, 1, 2))[..., None]).astype(
        jnp.bfloat16
    )
    attended = attended.reshape(per_owner_rows * tokens, kv_heads * group_heads * HEAD_DIM)
    head_part = jnp.dot(attended, w_out, preferred_element_type=jnp.float32)
    attn_sum = lax.psum(head_part.astype(jnp.bfloat16), "mlp").astype(jnp.float32)
    residual = wide_rows + attn_sum
    normed_two = (
        residual * lax.rsqrt(jnp.mean(residual * residual, axis=1, keepdims=True) + EPS) * mlp_gain
    ).astype(jnp.bfloat16)
    gate_out = jnp.dot(normed_two, w_gate, preferred_element_type=jnp.float32)
    up_out = jnp.dot(normed_two, w_up, preferred_element_type=jnp.float32)
    residual_share = lax.dynamic_slice_in_dim(residual, part_index * quarter, quarter, 1)
    hidden = (jax.nn.silu(gate_out) * up_out).astype(jnp.bfloat16)
    unit_part = jnp.dot(hidden, w_down, preferred_element_type=jnp.float32)
    unit_share = lax.psum_scatter(
        unit_part.astype(jnp.bfloat16), "mlp", scatter_dimension=1, tiled=True
    ).astype(jnp.float32)
    result = (residual_share + unit_share).astype(jnp.bfloat16)
    result_rows = result.reshape(per_owner_rows, tokens * quarter)
    returning = jnp.dot(receiver.T, result_rows, preferred_element_type=jnp.float32).astype(
        jnp.bfloat16
    )
    returning = returning.reshape(req_count, sends, tokens * quarter)
    arrived = lax.all_to_all(returning, "req", split_axis=0, concat_axis=0, tiled=True)
    back_rows = jnp.dot(
        sender.T,
        arrived.reshape(req_count * sends, tokens * quarter),
        preferred_element_type=jnp.float32,
    ).astype(jnp.bfloat16)
    return (back_rows.reshape(per_owner_rows, tokens, quarter), accepted_rows)


BF = jnp.bfloat16
F32 = jnp.float32
MESH = pl.DeviceIdType.MESH
LAST = (((1,), (1,)), ((), ()))


def layer_kernel(
    slot_of,
    lengths,
    parents,
    accepted,
    attn_gain,
    mlp_gain,
    drafts_hbm,
    cache_hbm,
    query_hbm,
    kv_hbm,
    out_hbm,
    gate_hbm,
    up_hbm,
    down_hbm,
    layer_ref,
    accepted_ref,
    drafts,
    cache,
    query_w,
    kv_w,
    out_w,
    gate_w,
    up_w,
    down_w,
    routed,
    gathered,
    fresh,
    attended,
    parts,
    pair_in,
    pair_out,
    far_in,
    rows_two,
    back,
    arrived,
    load_sem,
    route_s,
    route_r,
    core_s,
    core_r,
    far_s,
    far_r,
    pass_s,
    pass_r,
    pair_s,
    pair_r,
    cross_s,
    cross_r,
    two_s,
    two_r,
    back_s,
    back_r,
):
    count = lax.axis_size("req")
    groups = lax.axis_size("mlp")
    me = lax.axis_index("req")
    part = lax.axis_index("mlp")
    near, far, diagonal = part ^ 1, part ^ 2, part ^ 3
    tokens, quarter = drafts.shape[1], drafts.shape[2]
    per = drafts.shape[0]
    half = count // groups
    block = half * tokens
    total = per * tokens

    def place(source):
        return (source % groups) * half + source // groups

    loads = [
        pltpu.make_async_copy(src, dst, load_sem.at[i])
        for i, (src, dst) in enumerate(
            (
                (drafts_hbm, drafts),
                (query_hbm, query_w),
                (kv_hbm, kv_w),
                (cache_hbm, cache),
                (out_hbm, out_w),
                (gate_hbm, gate_w),
                (up_hbm, up_w),
                (down_hbm, down_w),
            )
        )
    ]
    for load in loads:
        load.start()

    barrier = pltpu.get_barrier_semaphore()
    for dr in range(count):
        for dm in range(groups):
            if dr or dm:
                pl.semaphore_signal(
                    barrier, inc=1, device_id=(me ^ dr, part ^ dm), device_id_type=MESH
                )

    owners = [slot_of[me * per + b] // per for b in range(per)]
    home = []
    for k in range(count):
        source = (k // half) + groups * (k % half)
        slot = jnp.int32(0)
        for b in range(per):
            s = slot_of[source * per + b]
            slot = jnp.where(s // per == me, s % per, slot)
        home.append(slot)

    loads[0].wait()
    for d in range(count):
        owner = me ^ d
        pick = jnp.int32(0)
        for b in range(per):
            pick = jnp.where(owners[b] == owner, b, pick)
        if d:
            routed[d] = drafts[pick]
        else:
            gathered[part, place(me)] = drafts[pick]

    pl.semaphore_wait(barrier, count * groups - 1)

    routes = []
    for d in range(1, count):
        copy = pltpu.make_async_remote_copy(
            src_ref=routed.at[d],
            dst_ref=gathered.at[part, place(me)],
            send_sem=route_s.at[d],
            recv_sem=route_r.at[d],
            device_id=(me ^ d, part),
            device_id_type=MESH,
        )
        copy.start()
        routes.append(copy)

    def spread(q, k, sends, recvs, d, target):
        return pltpu.make_async_remote_copy(
            src_ref=gathered.at[q, k],
            dst_ref=gathered.at[q, k],
            send_sem=sends.at[d],
            recv_sem=recvs.at[d],
            device_id=(me, target),
            device_id_type=MESH,
        )

    own = []
    for d in range(count):
        k = place(me ^ d)
        if d:
            routes[d - 1].wait_recv()
        across = spread(part, k, far_s, far_r, d, far)
        across.start()
        beside = spread(part, k, core_s, core_r, d, near)
        beside.start()
        own.append((across, beside))
    passed = []
    for d in range(count):
        k = place(me ^ d)
        own[d][0].wait_recv()
        copy = spread(far, k, pass_s, pass_r, d, near)
        copy.start()
        passed.append(copy)

    link = lax.broadcasted_iota(jnp.int32, (total, per), 0) // tokens
    lane = lax.broadcasted_iota(jnp.int32, (total, per), 1)
    slot_col = jnp.zeros((total, per), jnp.int32)
    for k in range(count):
        slot_col = jnp.where(link == k, home[k], slot_col)
    expand = (slot_col == lane).astype(BF)
    tree = jnp.dot(expand, parents[...].astype(F32).astype(BF), preferred_element_type=F32)
    row_t = lax.broadcasted_iota(jnp.int32, (total, tokens), 0) % tokens
    col_t = lax.broadcasted_iota(jnp.int32, (total, tokens), 1)
    parent = jnp.sum(jnp.where(row_t == col_t, tree, 0.0), axis=1, keepdims=True)
    row_i = lax.broadcasted_iota(jnp.int32, (total, total), 0)
    col_i = lax.broadcasted_iota(jnp.int32, (total, total), 1)
    target = parent.astype(jnp.int32) + (row_i // tokens) * tokens
    reach = jnp.where((col_i == target) | (row_i == col_i), 1.0, 0.0).astype(BF)
    for _ in range(max(tokens - 1, 1).bit_length()):
        reach = jnp.minimum(jnp.dot(reach, reach, preferred_element_type=F32), 1.0).astype(BF)
    visible = reach.astype(F32) > 0.5

    length_a = accepted.shape[1]
    rows_a = per * length_a
    slot_a = lax.broadcasted_iota(jnp.int32, (rows_a, per), 0) // length_a
    expand_a = (slot_a == lax.broadcasted_iota(jnp.int32, (rows_a, per), 1)).astype(BF)
    chosen = jnp.dot(expand_a, accepted[...].astype(F32).astype(BF), preferred_element_type=F32)
    pick_a = lax.broadcasted_iota(jnp.int32, (rows_a, length_a), 0) % length_a
    col_a = lax.broadcasted_iota(jnp.int32, (rows_a, length_a), 1)
    token = jnp.sum(jnp.where(pick_a == col_a, chosen, 0.0), axis=1, keepdims=True)
    row_s = lax.broadcasted_iota(jnp.int32, (rows_a, total), 0) // length_a
    base = jnp.zeros((rows_a, total), jnp.int32)
    for k in range(count):
        base = jnp.where(row_s == home[k], k * tokens, base)
    picker = (
        lax.broadcasted_iota(jnp.int32, (rows_a, total), 1) == base + token.astype(jnp.int32)
    ).astype(BF)

    for d in range(count):
        own[d][1].wait_recv()
    for d in range(count):
        passed[d].wait_recv()

    columns = [slice(q * quarter, (q + 1) * quarter) for q in range(groups)]
    wide = [gathered[q].reshape(total, quarter).astype(F32) for q in range(groups)]
    square = sum(jnp.sum(w * w, axis=1, keepdims=True) for w in wide)
    scale = lax.rsqrt(square / (groups * quarter) + EPS)
    normed = jnp.concatenate(
        [(w * scale * attn_gain[:, c]).astype(BF) for w, c in zip(wide, columns)], axis=1
    )
    loads[1].wait()
    loads[2].wait()
    query = lax.dot_general(normed, query_w[...], LAST, preferred_element_type=F32)
    query = query * (1.0 / math.sqrt(HEAD_DIM))
    fresh[...] = jnp.dot(normed, kv_w[...], preferred_element_type=F32).astype(BF)
    fresh_kv = fresh[...]
    accepted_ref[...] = jnp.dot(picker, fresh_kv, preferred_element_type=F32).astype(BF)

    width = 2 * HEAD_DIM
    low = lax.broadcasted_iota(jnp.int32, (total, width), 1) < HEAD_DIM
    first = query[:, :width]
    third = jnp.concatenate([query[:, width:], jnp.zeros((total, HEAD_DIM), F32)], axis=1)
    heads = [
        jnp.where(low, first, 0.0),
        jnp.where(low, pltpu.roll(first, HEAD_DIM, 1), 0.0),
        third,
    ]
    loads[3].wait()
    positions = cache.shape[1]
    col_c = lax.broadcasted_iota(jnp.int32, (len(heads) * tokens, positions), 1)
    low_t = lax.broadcasted_iota(jnp.int32, (tokens, width), 1) < HEAD_DIM
    for k in range(count):
        rows = slice(k * tokens, (k + 1) * tokens)
        q = jnp.concatenate([h[rows] for h in heads], axis=0)
        high = q.astype(BF)
        rest = q - high.astype(F32)
        mid = rest.astype(BF)
        last = (rest - mid.astype(F32)).astype(BF)
        stack = jnp.concatenate([high, mid, last], axis=0)
        held = cache[home[k]]
        n = q.shape[0]
        cached = lax.dot_general(stack, held, LAST, preferred_element_type=F32)
        cached = cached[:n] + cached[n : 2 * n] + cached[2 * n :]
        draft = lax.dot_general(stack, fresh_kv, LAST, preferred_element_type=F32)
        draft = draft[:n] + draft[n : 2 * n] + draft[2 * n :]
        cached = jnp.where(col_c < lengths[home[k]], cached, -jnp.inf)
        seen = visible[rows]
        draft = jnp.where(jnp.concatenate([seen] * len(heads), axis=0), draft, -jnp.inf)
        top = jnp.maximum(
            jnp.max(cached, axis=1, keepdims=True), jnp.max(draft, axis=1, keepdims=True)
        )
        weight_c = jnp.exp(cached - top).astype(BF)
        weight_d = jnp.exp(draft - top).astype(BF)
        bottom = jnp.sum(weight_c.astype(F32), axis=1, keepdims=True) + jnp.sum(
            weight_d.astype(F32), axis=1, keepdims=True
        )
        upper = jnp.dot(weight_c, held, preferred_element_type=F32) + jnp.dot(
            weight_d, fresh_kv, preferred_element_type=F32
        )
        result = upper / bottom
        a, b, c = (result[g * tokens : (g + 1) * tokens] for g in range(3))
        attended[rows, :width] = jnp.where(low_t, pltpu.roll(a, HEAD_DIM, 1), b).astype(BF)
        attended[rows, width:] = pltpu.roll(c, HEAD_DIM, 1)[:, :HEAD_DIM].astype(BF)

    def summed(stage):
        sends = []
        for i, piece in enumerate((diagonal, near)):
            copy = pltpu.make_async_remote_copy(
                src_ref=parts.at[stage, piece],
                dst_ref=pair_in.at[stage, i],
                send_sem=pair_s.at[stage, i],
                recv_sem=pair_r.at[stage, i],
                device_id=(me, near),
                device_id_type=MESH,
            )
            copy.start()
            sends.append(copy)
        sends[0].wait_recv()
        pair_out[stage] = (
            parts[stage, far].astype(F32) + pair_in[stage, 0].astype(F32)
        ).astype(BF)
        cross = pltpu.make_async_remote_copy(
            src_ref=pair_out.at[stage],
            dst_ref=far_in.at[stage],
            send_sem=cross_s.at[stage],
            recv_sem=cross_r.at[stage],
            device_id=(me, far),
            device_id_type=MESH,
        )
        cross.start()
        sends[1].wait_recv()
        mine = parts[stage, part].astype(F32) + pair_in[stage, 1].astype(F32)
        cross.wait_recv()
        return mine + far_in[stage].astype(F32), sends + [cross]

    loads[4].wait()
    product = jnp.dot(attended[...], out_w[...], preferred_element_type=F32)
    parts[0] = product.astype(BF).reshape(groups, block, groups * quarter)
    attn_sum, sends_one = summed(0)
    owned = jnp.concatenate(
        [
            gathered[q, pl.ds(part * half, half)].reshape(block, quarter).astype(F32)
            for q in range(groups)
        ],
        axis=1,
    )
    residual = owned + attn_sum
    mean = jnp.mean(residual * residual, axis=1, keepdims=True)
    rows_two[part] = (residual * lax.rsqrt(mean + EPS) * mlp_gain[...]).astype(BF)

    def share(q, i, to):
        copy = pltpu.make_async_remote_copy(
            src_ref=rows_two.at[q],
            dst_ref=rows_two.at[q],
            send_sem=two_s.at[i],
            recv_sem=two_r.at[i],
            device_id=(me, to),
            device_id_type=MESH,
        )
        copy.start()
        return copy

    two_far = share(part, 0, far)
    two_near = share(part, 1, near)
    loads[5].wait()
    loads[6].wait()
    loads[7].wait()
    two_far.wait_recv()
    two_pass = share(far, 2, near)
    two_near.wait_recv()
    two_pass.wait_recv()

    normed_two = rows_two[...].reshape(total, groups * quarter)
    gate = jnp.dot(normed_two, gate_w[...], preferred_element_type=F32)
    up = jnp.dot(normed_two, up_w[...], preferred_element_type=F32)
    hidden = (gate / (1.0 + jnp.exp(-gate)) * up).astype(BF)
    product = jnp.dot(hidden, down_w[...], preferred_element_type=F32)
    parts[1] = product.astype(BF).reshape(groups, block, groups * quarter)
    unit_sum, sends_two = summed(1)
    outcome = (residual + unit_sum).astype(BF)
    for j in range(half):
        for q in range(groups):
            back[j, q] = outcome[j * tokens : (j + 1) * tokens, q * quarter : (q + 1) * quarter]

    def give(j, i):
        source, q = part + groups * j, part ^ i
        return pltpu.make_async_remote_copy(
            src_ref=back.at[j, q],
            dst_ref=arrived.at[me],
            send_sem=back_s.at[j, i],
            recv_sem=back_r.at[me],
            device_id=(source, q),
            device_id_type=MESH,
        )

    for j in range(half):
        for i in range(groups):
            if i:
                give(j, i).start()
            else:

                @pl.when(part + groups * j != me)
                def _():
                    give(j, 0).start()

                @pl.when(part + groups * j == me)
                def _():
                    arrived[me] = back[j, part]

    def taken(o):
        return pltpu.make_async_remote_copy(
            src_ref=back.at[0, 0],
            dst_ref=arrived.at[o],
            send_sem=back_s.at[0, 0],
            recv_sem=back_r.at[o],
            device_id=(me, near),
            device_id_type=MESH,
        )

    for d in range(count):
        if d:
            taken(me ^ d).wait_recv()
        else:

            @pl.when(me % groups != part)
            def _():
                taken(me).wait_recv()

    for b in range(per):
        layer_ref[b] = arrived[owners[b]]

    for copy in routes + [c for pair in own for c in pair] + passed:
        copy.wait_send()
    for copy in sends_one + sends_two + [two_far, two_near, two_pass]:
        copy.wait_send()
    for j in range(half):
        for i in range(groups):
            if i:
                give(j, i).wait_send()
            else:

                @pl.when(part + groups * j != me)
                def _():
                    give(j, 0).wait_send()


def fused(
    drafts,
    slot_of,
    lengths,
    parents,
    accepted_tokens,
    cached_key_value,
    attn_gain,
    query_weight,
    key_value_weight,
    w_out,
    mlp_gain,
    w_gate,
    w_up,
    w_down,
):
    count = lax.axis_size("req")
    groups = lax.axis_size("mlp")
    per, tokens, quarter = drafts.shape
    accept = accepted_tokens.shape[1]
    positions, width = cached_key_value.shape[1], cached_key_value.shape[3]
    model = groups * quarter
    half = count // groups
    block = half * tokens
    total = per * tokens
    span = query_weight.shape[1]
    units = w_gate.shape[1]
    smem = pl.BlockSpec(memory_space=pltpu.SMEM)
    vmem = pl.BlockSpec(memory_space=pltpu.VMEM)
    hbm = pl.BlockSpec(memory_space=pl.ANY)
    dma = pltpu.SemaphoreType.DMA
    out, taken = pl.pallas_call(
        layer_kernel,
        out_shape=(
            jax.ShapeDtypeStruct((per, tokens, quarter), BF),
            jax.ShapeDtypeStruct((per * accept, width), BF),
        ),
        in_specs=[smem, smem, vmem, vmem, vmem, vmem] + [hbm] * 8,
        out_specs=(vmem, vmem),
        scratch_shapes=[
            pltpu.VMEM((per, tokens, quarter), BF),
            pltpu.VMEM((per, positions, width), BF),
            pltpu.VMEM((span, model), BF),
            pltpu.VMEM((model, width), BF),
            pltpu.VMEM((span, model), BF),
            pltpu.VMEM((model, units), BF),
            pltpu.VMEM((model, units), BF),
            pltpu.VMEM((units, model), BF),
            pltpu.VMEM((count, tokens, quarter), BF),
            pltpu.VMEM((groups, count, tokens, quarter), BF),
            pltpu.VMEM((total, width), BF),
            pltpu.VMEM((total, span), BF),
            pltpu.VMEM((2, groups, block, model), BF),
            pltpu.VMEM((2, 2, block, model), BF),
            pltpu.VMEM((2, block, model), BF),
            pltpu.VMEM((2, block, model), BF),
            pltpu.VMEM((groups, block, model), BF),
            pltpu.VMEM((half, groups, tokens, quarter), BF),
            pltpu.VMEM((count, tokens, quarter), BF),
            dma((8,)),
            dma((count,)),
            dma((count,)),
            dma((count,)),
            dma((count,)),
            dma((count,)),
            dma((count,)),
            dma((count,)),
            dma((count,)),
            dma((2, 2)),
            dma((2, 2)),
            dma((2,)),
            dma((2,)),
            dma((3,)),
            dma((3,)),
            dma((half, groups)),
            dma((count,)),
        ],
        compiler_params=pltpu.CompilerParams(
            collective_id=0, has_side_effects=True, vmem_limit_bytes=48 * 1024 * 1024
        ),
    )(
        slot_of,
        lengths,
        parents,
        accepted_tokens,
        attn_gain.reshape(1, model),
        mlp_gain.reshape(1, model),
        drafts,
        cached_key_value.reshape(per, positions, width),
        query_weight.T,
        key_value_weight,
        w_out,
        w_gate,
        w_up,
        w_down,
    )
    return (out, taken.reshape(per, accept, 1, width))


def body(*args):
    drafts, cached_key_value = args[0], args[5]
    count, groups = lax.axis_size("req"), lax.axis_size("mlp")
    one_each = count == drafts.shape[0] and count % groups == 0 and groups == 4
    three_heads = args[7].shape[1] == 3 * HEAD_DIM and cached_key_value.shape[2] == 1
    return (fused if one_each and three_heads else per_device)(*args)


def solution(mesh):
    placed = (
        P("req", None, "mlp"),
        P(),
        P("req"),
        P("req", None),
        P("req", None),
        P("req", None, "mlp", None),
        P(),
        P(None, "mlp"),
        P(None, "mlp"),
        P("mlp", None),
        P(),
        P(None, "mlp"),
        P(None, "mlp"),
        P("mlp", None),
    )
    return jax.shard_map(
        body,
        mesh=mesh,
        in_specs=placed,
        out_specs=(P("req", None, "mlp"), P("req", None, "mlp", None)),
        check_vma=False,
    )
```

```python
import math

import jax
import jax.numpy as jnp
from jax import lax
from jax.experimental import pallas as pl
from jax.experimental.pallas import tpu as pltpu
from jax.sharding import PartitionSpec as P

HEAD_DIM = 64


EPS = 1e-06
HIGH = lax.Precision.HIGHEST


def route_tables(slot_of, per_owner_rows, sources, groups, my_index):
    owners = slot_of // per_owner_rows
    owner_grid = owners.reshape(sources, per_owner_rows)
    request_ids = jnp.arange(per_owner_rows)
    earlier = request_ids[None, :] < request_ids[:, None]
    position = jnp.sum((owner_grid[:, :, None] == owner_grid[:, None, :]) & earlier[None], axis=2)
    column = (jnp.arange(sources, dtype=jnp.int32)[:, None] * groups + position).reshape(-1)
    slot_count = sources * groups
    my_owners = lax.dynamic_index_in_dim(owner_grid, my_index, 0, keepdims=False)
    my_position = lax.dynamic_index_in_dim(position, my_index, 0, keepdims=False)
    target = my_owners * groups + my_position
    sender = (jnp.arange(slot_count)[:, None] == target[None, :]).astype(jnp.bfloat16)
    arrive = (slot_of[None, :] == my_index * per_owner_rows + request_ids[:, None]).astype(
        jnp.bfloat16
    )
    places = (column[:, None] == jnp.arange(slot_count)[None, :]).astype(jnp.bfloat16)
    receiver = jnp.dot(arrive, places, preferred_element_type=jnp.float32).astype(jnp.bfloat16)
    return (sender, receiver)


def ancestry(tree_links, tokens):
    parent_link = (
        tree_links[:, :, None] == jnp.arange(tokens, dtype=jnp.int32)[None, None, :]
    ).astype(jnp.float32)
    reachable = jnp.maximum(parent_link, jnp.eye(tokens, dtype=jnp.float32)[None])
    for squaring in range(max(tokens - 1, 1).bit_length()):
        reachable = jnp.minimum(
            jnp.einsum("rij,rjk->rik", reachable, reachable, precision=HIGH), 1.0
        )
    return reachable > 0.5


def cache_scores(query_rows, cache_block, cache_len, score_scale, head_size):
    key_rows = cache_block[..., :head_size].astype(jnp.float32)
    scores = jnp.einsum("rtkgd,rckd->rkgtc", query_rows, key_rows, precision=HIGH) * score_scale
    row_ids = jnp.arange(cache_block.shape[1])
    live_rows = row_ids[None, :] < cache_len[:, None]
    return jnp.where(live_rows[:, None, None, None, :], scores, -jnp.inf)


def weighted(weights, cache_block, head_size):
    return jnp.einsum(
        "rkgtc,rckd->rtkgd",
        weights,
        cache_block[..., head_size:],
        preferred_element_type=jnp.float32,
    )


def per_device(
    drafts,
    slot_of,
    lengths,
    parents,
    accepted_tokens,
    cached_key_value,
    attn_gain,
    query_weight,
    key_value_weight,
    w_out,
    mlp_gain,
    w_gate,
    w_up,
    w_down,
):
    req_count = lax.axis_size("req")
    my_index = lax.axis_index("req")
    part_index = lax.axis_index("mlp")
    per_owner_rows, tokens, quarter = drafts.shape
    sends = max(1, per_owner_rows // req_count)
    sender, receiver = route_tables(slot_of, per_owner_rows, req_count, sends, my_index)
    flat_rows = drafts.reshape(per_owner_rows, tokens * quarter)
    outgoing = jnp.dot(sender, flat_rows, preferred_element_type=jnp.float32).astype(jnp.bfloat16)
    outgoing = outgoing.reshape(req_count, sends, tokens * quarter)
    incoming = lax.all_to_all(outgoing, "req", split_axis=0, concat_axis=0, tiled=True)
    local_rows = jnp.dot(
        receiver,
        incoming.reshape(req_count * sends, tokens * quarter),
        preferred_element_type=jnp.float32,
    ).astype(jnp.bfloat16)
    local_rows = local_rows.reshape(per_owner_rows * tokens, quarter)
    full_rows = lax.all_gather(local_rows, "mlp", axis=1, tiled=True)
    wide_rows = full_rows.astype(jnp.float32)
    normalized_rows = (
        wide_rows
        * lax.rsqrt(jnp.mean(wide_rows * wide_rows, axis=1, keepdims=True) + EPS)
        * attn_gain
    ).astype(jnp.bfloat16)
    kv_heads = key_value_weight.shape[1] // (2 * HEAD_DIM)
    group_heads = query_weight.shape[1] // (kv_heads * HEAD_DIM)
    query_rows = jnp.dot(normalized_rows, query_weight, preferred_element_type=jnp.float32).reshape(
        per_owner_rows, tokens, kv_heads, group_heads, HEAD_DIM
    )
    new_key_value = (
        jnp.dot(normalized_rows, key_value_weight, preferred_element_type=jnp.float32)
        .astype(jnp.bfloat16)
        .reshape(per_owner_rows, tokens, kv_heads, 2 * HEAD_DIM)
    )
    picker = (
        accepted_tokens[:, :, None] == jnp.arange(tokens, dtype=jnp.int32)[None, None, :]
    ).astype(jnp.bfloat16)
    accepted_rows = jnp.einsum(
        "rat,rtkd->rakd", picker, new_key_value, preferred_element_type=jnp.float32
    ).astype(jnp.bfloat16)
    score_scale = 1.0 / math.sqrt(HEAD_DIM)
    draft_keys = new_key_value[..., :HEAD_DIM].astype(jnp.float32)
    draft_scores = (
        jnp.einsum("rtkgd,rjkd->rkgtj", query_rows, draft_keys, precision=HIGH) * score_scale
    )
    draft_scores = jnp.where(ancestry(parents, tokens)[:, None, None], draft_scores, -jnp.inf)
    draft_top = jnp.max(draft_scores, axis=-1)
    scores = cache_scores(query_rows, cached_key_value, lengths, score_scale, HEAD_DIM)
    row_top = jnp.maximum(draft_top, jnp.max(scores, axis=-1))
    weights = jnp.exp(scores - row_top[..., None]).astype(jnp.bfloat16)
    numerator = weighted(weights, cached_key_value, HEAD_DIM)
    denominator = jnp.sum(weights.astype(jnp.float32), axis=-1)
    draft_weights = jnp.exp(draft_scores - row_top[..., None]).astype(jnp.bfloat16)
    numerator = numerator + jnp.einsum(
        "rkgtj,rjkd->rtkgd",
        draft_weights,
        new_key_value[..., HEAD_DIM:],
        preferred_element_type=jnp.float32,
    )
    denominator = denominator + jnp.sum(draft_weights.astype(jnp.float32), axis=-1)
    attended = (numerator / jnp.transpose(denominator, (0, 3, 1, 2))[..., None]).astype(
        jnp.bfloat16
    )
    attended = attended.reshape(per_owner_rows * tokens, kv_heads * group_heads * HEAD_DIM)
    head_part = jnp.dot(attended, w_out, preferred_element_type=jnp.float32)
    attn_sum = lax.psum(head_part.astype(jnp.bfloat16), "mlp").astype(jnp.float32)
    residual = wide_rows + attn_sum
    normed_two = (
        residual * lax.rsqrt(jnp.mean(residual * residual, axis=1, keepdims=True) + EPS) * mlp_gain
    ).astype(jnp.bfloat16)
    gate_out = jnp.dot(normed_two, w_gate, preferred_element_type=jnp.float32)
    up_out = jnp.dot(normed_two, w_up, preferred_element_type=jnp.float32)
    residual_share = lax.dynamic_slice_in_dim(residual, part_index * quarter, quarter, 1)
    hidden = (jax.nn.silu(gate_out) * up_out).astype(jnp.bfloat16)
    unit_part = jnp.dot(hidden, w_down, preferred_element_type=jnp.float32)
    unit_share = lax.psum_scatter(
        unit_part.astype(jnp.bfloat16), "mlp", scatter_dimension=1, tiled=True
    ).astype(jnp.float32)
    result = (residual_share + unit_share).astype(jnp.bfloat16)
    result_rows = result.reshape(per_owner_rows, tokens * quarter)
    returning = jnp.dot(receiver.T, result_rows, preferred_element_type=jnp.float32).astype(
        jnp.bfloat16
    )
    returning = returning.reshape(req_count, sends, tokens * quarter)
    arrived = lax.all_to_all(returning, "req", split_axis=0, concat_axis=0, tiled=True)
    back_rows = jnp.dot(
        sender.T,
        arrived.reshape(req_count * sends, tokens * quarter),
        preferred_element_type=jnp.float32,
    ).astype(jnp.bfloat16)
    return (back_rows.reshape(per_owner_rows, tokens, quarter), accepted_rows)


BF = jnp.bfloat16
F32 = jnp.float32
MESH = pl.DeviceIdType.MESH
LAST = (((1,), (1,)), ((), ()))


def layer_kernel(
    slot_hbm,
    lengths_hbm,
    parents_hbm,
    accepted_hbm,
    attn_gain_hbm,
    mlp_gain_hbm,
    drafts_hbm,
    cache_hbm,
    query_hbm,
    kv_hbm,
    out_hbm,
    gate_hbm,
    up_hbm,
    down_hbm,
    layer_ref,
    accepted_ref,
    slot_of,
    lengths,
    parents,
    accepted,
    attn_gain,
    mlp_gain,
    drafts,
    cache,
    query_w,
    kv_w,
    out_w,
    gate_w,
    up_w,
    down_w,
    routed,
    gathered,
    fresh,
    attended,
    rows_one,
    one_in,
    one_out,
    one_far,
    rows_two,
    parts,
    pair_in,
    pair_out,
    far_in,
    back,
    arrived,
    load_sem,
    route_s,
    route_r,
    core_s,
    core_r,
    far_s,
    far_r,
    pass_s,
    pass_r,
    pair_s,
    pair_r,
    cross_s,
    cross_r,
    one_s,
    one_r,
    over_s,
    over_r,
    two_s,
    two_r,
    back_s,
    back_r,
):
    count = lax.axis_size("req")
    groups = lax.axis_size("mlp")
    me = lax.axis_index("req")
    part = lax.axis_index("mlp")
    near, far, diagonal = part ^ 1, part ^ 2, part ^ 3
    tokens, quarter = drafts.shape[1], drafts.shape[2]
    per = drafts.shape[0]
    total = per * tokens

    loads = [
        pltpu.make_async_copy(src, dst, load_sem.at[i])
        for i, (src, dst) in enumerate(
            (
                (drafts_hbm, drafts),
                (query_hbm, query_w),
                (kv_hbm, kv_w),
                (cache_hbm, cache),
                (out_hbm, out_w),
                (gate_hbm, gate_w),
                (up_hbm, up_w),
                (down_hbm, down_w),
                (slot_hbm, slot_of),
                (lengths_hbm, lengths),
                (parents_hbm, parents),
                (accepted_hbm, accepted),
                (attn_gain_hbm, attn_gain),
                (mlp_gain_hbm, mlp_gain),
            )
        )
    ]
    for i in (8, 0, 9, 10, 11, 12, 13, 1, 2, 3, 4, 5, 6, 7):
        loads[i].start()

    barrier = pltpu.get_barrier_semaphore()
    for d in range(1, count):
        pl.semaphore_signal(barrier, inc=1, device_id=(me ^ d, part), device_id_type=MESH)
    for d in range(1, groups):
        pl.semaphore_signal(barrier, inc=1, device_id=(me, part ^ d), device_id_type=MESH)

    loads[8].wait()
    owners = [slot_of[me * per + b] // per for b in range(per)]
    home = []
    for k in range(count):
        slot = jnp.int32(0)
        for b in range(per):
            s = slot_of[k * per + b]
            slot = jnp.where(s // per == me, s % per, slot)
        home.append(slot)

    loads[0].wait()
    for d in range(count):
        owner = me ^ d
        pick = jnp.int32(0)
        for b in range(per):
            pick = jnp.where(owners[b] == owner, b, pick)
        if d:
            routed[d] = drafts[pick]
        else:
            gathered[part, me] = drafts[pick]

    pl.semaphore_wait(barrier, count + groups - 2)

    routes = []
    for d in range(1, count):
        copy = pltpu.make_async_remote_copy(
            src_ref=routed.at[d],
            dst_ref=gathered.at[part, me],
            send_sem=route_s.at[d],
            recv_sem=route_r.at[d],
            device_id=(me ^ d, part),
            device_id_type=MESH,
        )
        copy.start()
        routes.append(copy)

    def spread(q, k, sends, recvs, d, target):
        return pltpu.make_async_remote_copy(
            src_ref=gathered.at[q, k],
            dst_ref=gathered.at[q, k],
            send_sem=sends.at[d],
            recv_sem=recvs.at[d],
            device_id=(me, target),
            device_id_type=MESH,
        )

    pending = list(routes)
    own = []
    for d in range(count):
        k = me ^ d
        if d:
            routes[d - 1].wait_recv()
        across = spread(part, k, far_s, far_r, d, far)
        across.start()
        beside = spread(part, k, core_s, core_r, d, near)
        beside.start()
        own.append((across, beside))
        pending += [across, beside]
    passed = []
    for d in range(count):
        k = me ^ d
        own[d][0].wait_recv()
        copy = spread(far, k, pass_s, pass_r, d, near)
        copy.start()
        passed.append(copy)
        pending.append(copy)

    for i in (9, 10, 11, 12, 13):
        loads[i].wait()
    link = lax.broadcasted_iota(jnp.int32, (total, per), 0) // tokens
    lane = lax.broadcasted_iota(jnp.int32, (total, per), 1)
    slot_col = jnp.zeros((total, per), jnp.int32)
    for k in range(count):
        slot_col = jnp.where(link == k, home[k], slot_col)
    expand = (slot_col == lane).astype(BF)
    tree = jnp.dot(expand, parents[...].astype(F32).astype(BF), preferred_element_type=F32)
    row_t = lax.broadcasted_iota(jnp.int32, (total, tokens), 0) % tokens
    col_t = lax.broadcasted_iota(jnp.int32, (total, tokens), 1)
    parent = jnp.sum(jnp.where(row_t == col_t, tree, 0.0), axis=1, keepdims=True)
    row_i = lax.broadcasted_iota(jnp.int32, (total, total), 0)
    col_i = lax.broadcasted_iota(jnp.int32, (total, total), 1)
    target = parent.astype(jnp.int32) + (row_i // tokens) * tokens
    reach = jnp.where((col_i == target) | (row_i == col_i), 1.0, 0.0).astype(BF)
    for _ in range(max(tokens - 1, 1).bit_length()):
        reach = jnp.minimum(jnp.dot(reach, reach, preferred_element_type=F32), 1.0).astype(BF)
    visible = reach.astype(F32) > 0.5

    length_a = accepted.shape[1]
    rows_a = per * length_a
    slot_a = lax.broadcasted_iota(jnp.int32, (rows_a, per), 0) // length_a
    expand_a = (slot_a == lax.broadcasted_iota(jnp.int32, (rows_a, per), 1)).astype(BF)
    chosen = jnp.dot(expand_a, accepted[...].astype(F32).astype(BF), preferred_element_type=F32)
    pick_a = lax.broadcasted_iota(jnp.int32, (rows_a, length_a), 0) % length_a
    col_a = lax.broadcasted_iota(jnp.int32, (rows_a, length_a), 1)
    token = jnp.sum(jnp.where(pick_a == col_a, chosen, 0.0), axis=1, keepdims=True)
    row_s = lax.broadcasted_iota(jnp.int32, (rows_a, total), 0) // length_a
    base = jnp.zeros((rows_a, total), jnp.int32)
    for k in range(count):
        base = jnp.where(row_s == home[k], k * tokens, base)
    picker = (
        lax.broadcasted_iota(jnp.int32, (rows_a, total), 1) == base + token.astype(jnp.int32)
    ).astype(BF)

    for d in range(count):
        own[d][1].wait_recv()
    for d in range(count):
        passed[d].wait_recv()

    columns = [slice(q * quarter, (q + 1) * quarter) for q in range(groups)]
    wide = [gathered[q].reshape(total, quarter).astype(F32) for q in range(groups)]
    square = sum(jnp.sum(w * w, axis=1, keepdims=True) for w in wide)
    scale = lax.rsqrt(square / (groups * quarter) + EPS)
    normed = jnp.concatenate(
        [(w * scale * attn_gain[:, c]).astype(BF) for w, c in zip(wide, columns)], axis=1
    )
    loads[1].wait()
    loads[2].wait()
    query = lax.dot_general(normed, query_w[...], LAST, preferred_element_type=F32)
    query = query * (1.0 / math.sqrt(HEAD_DIM))
    fresh[...] = jnp.dot(normed, kv_w[...], preferred_element_type=F32).astype(BF)
    fresh_kv = fresh[...]
    accepted_ref[...] = jnp.dot(picker, fresh_kv, preferred_element_type=F32).astype(BF)

    width = 2 * HEAD_DIM
    low = lax.broadcasted_iota(jnp.int32, (total, width), 1) < HEAD_DIM
    first = query[:, :width]
    third = jnp.concatenate([query[:, width:], jnp.zeros((total, HEAD_DIM), F32)], axis=1)
    heads = [
        jnp.where(low, first, 0.0),
        jnp.where(low, pltpu.roll(first, HEAD_DIM, 1), 0.0),
        third,
    ]
    loads[3].wait()
    positions = cache.shape[1]
    col_c = lax.broadcasted_iota(jnp.int32, (len(heads) * tokens, positions), 1)
    low_t = lax.broadcasted_iota(jnp.int32, (tokens, width), 1) < HEAD_DIM
    for k in range(count):
        rows = slice(k * tokens, (k + 1) * tokens)
        q = jnp.concatenate([h[rows] for h in heads], axis=0)
        high = q.astype(BF)
        rest = q - high.astype(F32)
        mid = rest.astype(BF)
        last = (rest - mid.astype(F32)).astype(BF)
        stack = jnp.concatenate([high, mid, last], axis=0)
        held = cache[home[k]]
        n = q.shape[0]
        cached = lax.dot_general(stack, held, LAST, preferred_element_type=F32)
        cached = cached[:n] + cached[n : 2 * n] + cached[2 * n :]
        draft = lax.dot_general(stack, fresh_kv, LAST, preferred_element_type=F32)
        draft = draft[:n] + draft[n : 2 * n] + draft[2 * n :]
        cached = jnp.where(col_c < lengths[home[k]], cached, -jnp.inf)
        seen = visible[rows]
        draft = jnp.where(jnp.concatenate([seen] * len(heads), axis=0), draft, -jnp.inf)
        top = jnp.maximum(
            jnp.max(cached, axis=1, keepdims=True), jnp.max(draft, axis=1, keepdims=True)
        )
        weight_c = jnp.exp(cached - top).astype(BF)
        weight_d = jnp.exp(draft - top).astype(BF)
        bottom = jnp.sum(weight_c.astype(F32), axis=1, keepdims=True) + jnp.sum(
            weight_d.astype(F32), axis=1, keepdims=True
        )
        upper = jnp.dot(weight_c, held, preferred_element_type=F32) + jnp.dot(
            weight_d, fresh_kv, preferred_element_type=F32
        )
        result = upper / bottom
        a, b, c = (result[g * tokens : (g + 1) * tokens] for g in range(3))
        attended[rows, :width] = jnp.where(low_t, pltpu.roll(a, HEAD_DIM, 1), b).astype(BF)
        attended[rows, width:] = pltpu.roll(c, HEAD_DIM, 1)[:, :HEAD_DIM].astype(BF)

    loads[4].wait()
    chunks = parts.shape[0]
    step = total // chunks

    def send(src, dst, sends, recvs, to):
        copy = pltpu.make_async_remote_copy(
            src_ref=src,
            dst_ref=dst,
            send_sem=sends,
            recv_sem=recvs,
            device_id=(me, to),
            device_id_type=MESH,
        )
        copy.start()
        pending.append(copy)
        return copy

    heads_all = attended[...]
    ahead, after, over = [], [], []
    for c in range(groups):
        product = jnp.dot(heads_all, out_w[:, columns[c]], preferred_element_type=F32)
        rows_one[c] = product.astype(BF).reshape(groups, step, quarter)
        for i, piece, out in ((0, diagonal, ahead), (1, near, after)):
            out.append(
                send(
                    rows_one.at[c, piece],
                    one_in.at[c, i],
                    one_s.at[c, i],
                    one_r.at[c, i],
                    near,
                )
            )
    for c in range(groups):
        ahead[c].wait_recv()
        one_out[c] = (rows_one[c, far].astype(F32) + one_in[c, 0].astype(F32)).astype(BF)
        over.append(send(one_out.at[c], one_far.at[c], over_s.at[c], over_r.at[c], far))
    attn, residual = [], []
    mine_rows = count // groups
    for c in range(groups):
        after[c].wait_recv()
        term = rows_one[c, part].astype(F32) + one_in[c, 1].astype(F32)
        over[c].wait_recv()
        attn.append(term + one_far[c].astype(F32))
        owned = gathered[c, pl.ds(part * mine_rows, mine_rows)].reshape(step, quarter)
        residual.append(owned.astype(F32) + attn[c])
    square = sum(jnp.sum(r * r, axis=1, keepdims=True) for r in residual)
    scale = lax.rsqrt(square / (groups * quarter) + EPS)
    shared = []
    for c in range(groups):
        rows_two[c, part] = (residual[c] * scale * mlp_gain[:, columns[c]]).astype(BF)
        mine = rows_two.at[c, part]
        shared.append(
            (
                send(mine, mine, two_s.at[0, c], two_r.at[0, c], far),
                send(mine, mine, two_s.at[1, c], two_r.at[1, c], near),
            )
        )
    relayed = []
    for c in range(groups):
        shared[c][0].wait_recv()
        other = rows_two.at[c, far]
        relayed.append(send(other, other, two_s.at[2, c], two_r.at[2, c], near))
    for c in range(groups):
        shared[c][1].wait_recv()
        relayed[c].wait_recv()
    normed_two = jnp.concatenate(
        [rows_two[c].reshape(total, quarter) for c in range(groups)], axis=1
    )
    loads[5].wait()
    loads[6].wait()
    loads[7].wait()
    gate = jnp.dot(normed_two, gate_w[...], preferred_element_type=F32)
    up = jnp.dot(normed_two, up_w[...], preferred_element_type=F32)
    hidden = (gate / (1.0 + jnp.exp(-gate)) * up).astype(BF)

    each = count // chunks
    product = jnp.dot(hidden, down_w[...], preferred_element_type=F32)
    for q in range(groups):
        for c in range(chunks):
            term = product[c * step : (c + 1) * step, columns[q]]
            parts[c, q] = (term + jnp.where(part == c, attn[q], 0.0)).astype(BF)

    def pair(c, i, piece):
        copy = pltpu.make_async_remote_copy(
            src_ref=parts.at[c, piece],
            dst_ref=pair_in.at[c, i],
            send_sem=pair_s.at[c, i],
            recv_sem=pair_r.at[c, i],
            device_id=(me, near),
            device_id_type=MESH,
        )
        copy.start()
        pending.append(copy)
        return copy

    pairs = [pair(c, 0, diagonal) for c in range(chunks)]
    mines = [pair(c, 1, near) for c in range(chunks)]
    crossed = []
    for c in range(chunks):
        pairs[c].wait_recv()
        pair_out[c] = (parts[c, far].astype(F32) + pair_in[c, 0].astype(F32)).astype(BF)
        copy = pltpu.make_async_remote_copy(
            src_ref=pair_out.at[c],
            dst_ref=far_in.at[c],
            send_sem=cross_s.at[c],
            recv_sem=cross_r.at[c],
            device_id=(me, far),
            device_id_type=MESH,
        )
        copy.start()
        crossed.append(copy)
    pending += crossed

    def give(k):
        return pltpu.make_async_remote_copy(
            src_ref=back.at[k],
            dst_ref=arrived.at[me],
            send_sem=back_s.at[k],
            recv_sem=back_r.at[me],
            device_id=(k, part),
            device_id_type=MESH,
        )

    for c in range(chunks):
        mines[c].wait_recv()
        owned = gathered[part, c * each : (c + 1) * each].reshape(step, quarter)
        mine = owned.astype(F32) + parts[c, part].astype(F32)
        mine = mine + pair_in[c, 1].astype(F32)
        crossed[c].wait_recv()
        outcome = (mine + far_in[c].astype(F32)).astype(BF)
        for j in range(each):
            k = c * each + j
            back[k] = outcome[j * tokens : (j + 1) * tokens]

            @pl.when(me != k)
            def _(k=k):
                give(k).start()

            @pl.when(me == k)
            def _(k=k):
                arrived[k] = back[k]

    def taken(o):
        return pltpu.make_async_remote_copy(
            src_ref=back.at[0],
            dst_ref=arrived.at[o],
            send_sem=back_s.at[0],
            recv_sem=back_r.at[o],
            device_id=(me, near),
            device_id_type=MESH,
        )

    for d in range(1, count):
        taken(me ^ d).wait_recv()

    for b in range(per):
        layer_ref[b] = arrived[owners[b]]

    for copy in pending:
        copy.wait_send()
    for k in range(count):

        @pl.when(me != k)
        def _(k=k):
            give(k).wait_send()


def fused(
    drafts,
    slot_of,
    lengths,
    parents,
    accepted_tokens,
    cached_key_value,
    attn_gain,
    query_weight,
    key_value_weight,
    w_out,
    mlp_gain,
    w_gate,
    w_up,
    w_down,
):
    count = lax.axis_size("req")
    groups = lax.axis_size("mlp")
    per, tokens, quarter = drafts.shape
    accept = accepted_tokens.shape[1]
    positions, width = cached_key_value.shape[1], cached_key_value.shape[3]
    model = groups * quarter
    chunks = 4
    step = per * tokens // chunks
    total = per * tokens
    span = query_weight.shape[1]
    units = w_gate.shape[1]
    vmem = pl.BlockSpec(memory_space=pltpu.VMEM)
    hbm = pl.BlockSpec(memory_space=pltpu.HBM)
    dma = pltpu.SemaphoreType.DMA
    out, taken = pl.pallas_call(
        layer_kernel,
        out_shape=(
            jax.ShapeDtypeStruct((per, tokens, quarter), BF),
            jax.ShapeDtypeStruct((per * accept, width), BF),
        ),
        in_specs=[hbm] * 14,
        out_specs=(vmem, vmem),
        scratch_shapes=[
            pltpu.SMEM(slot_of.shape, jnp.int32),
            pltpu.SMEM(lengths.shape, jnp.int32),
            pltpu.VMEM(parents.shape, jnp.int32),
            pltpu.VMEM(accepted_tokens.shape, jnp.int32),
            pltpu.VMEM((1, model), F32),
            pltpu.VMEM((1, model), F32),
            pltpu.VMEM((per, tokens, quarter), BF),
            pltpu.VMEM((per, positions, width), BF),
            pltpu.VMEM((span, model), BF),
            pltpu.VMEM((model, width), BF),
            pltpu.VMEM((span, model), BF),
            pltpu.VMEM((model, units), BF),
            pltpu.VMEM((model, units), BF),
            pltpu.VMEM((units, model), BF),
            pltpu.VMEM((count, tokens, quarter), BF),
            pltpu.VMEM((groups, count, tokens, quarter), BF),
            pltpu.VMEM((total, width), BF),
            pltpu.VMEM((total, span), BF),
            pltpu.VMEM((groups, groups, step, quarter), BF),
            pltpu.VMEM((groups, 2, step, quarter), BF),
            pltpu.VMEM((groups, step, quarter), BF),
            pltpu.VMEM((groups, step, quarter), BF),
            pltpu.VMEM((groups, groups, step, quarter), BF),
            pltpu.VMEM((chunks, groups, step, quarter), BF),
            pltpu.VMEM((chunks, 2, step, quarter), BF),
            pltpu.VMEM((chunks, step, quarter), BF),
            pltpu.VMEM((chunks, step, quarter), BF),
            pltpu.VMEM((count, tokens, quarter), BF),
            pltpu.VMEM((count, tokens, quarter), BF),
            dma((14,)),
            dma((count,)),
            dma((count,)),
            dma((count,)),
            dma((count,)),
            dma((count,)),
            dma((count,)),
            dma((count,)),
            dma((count,)),
            dma((chunks, 2)),
            dma((chunks, 2)),
            dma((chunks,)),
            dma((chunks,)),
            dma((groups, 2)),
            dma((groups, 2)),
            dma((groups,)),
            dma((groups,)),
            dma((3, groups)),
            dma((3, groups)),
            dma((count,)),
            dma((count,)),
        ],
        compiler_params=pltpu.CompilerParams(
            collective_id=0, has_side_effects=True, vmem_limit_bytes=60 * 1024 * 1024
        ),
    )(
        slot_of,
        lengths,
        parents,
        accepted_tokens,
        attn_gain.reshape(1, model),
        mlp_gain.reshape(1, model),
        drafts,
        cached_key_value.reshape(per, positions, width),
        query_weight.T,
        key_value_weight,
        w_out,
        w_gate,
        w_up,
        w_down,
    )
    return (out, taken.reshape(per, accept, 1, width))


def body(*args):
    drafts, cached_key_value = args[0], args[5]
    count, groups = lax.axis_size("req"), lax.axis_size("mlp")
    one_each = count == drafts.shape[0] == 8 and groups == 4
    three_heads = args[7].shape[1] == 3 * HEAD_DIM and cached_key_value.shape[2] == 1
    return (fused if one_each and three_heads else per_device)(*args)


def solution(mesh):
    placed = (
        P("req", None, "mlp"),
        P(),
        P("req"),
        P("req", None),
        P("req", None),
        P("req", None, "mlp", None),
        P(),
        P(None, "mlp"),
        P(None, "mlp"),
        P("mlp", None),
        P(),
        P(None, "mlp"),
        P(None, "mlp"),
        P("mlp", None),
    )
    return jax.shard_map(
        body,
        mesh=mesh,
        in_specs=placed,
        out_specs=(P("req", None, "mlp"), P("req", None, "mlp", None)),
        check_vma=False,
    )
```

```python
import math

import jax
import jax.numpy as jnp
from jax import lax
from jax.experimental import pallas as pl
from jax.experimental.pallas import tpu as pltpu
from jax.sharding import PartitionSpec as P

HEAD_DIM = 64


EPS = 1e-06
HIGH = lax.Precision.HIGHEST


def route_tables(slot_of, per_owner_rows, sources, groups, my_index):
    owners = slot_of // per_owner_rows
    owner_grid = owners.reshape(sources, per_owner_rows)
    request_ids = jnp.arange(per_owner_rows)
    earlier = request_ids[None, :] < request_ids[:, None]
    position = jnp.sum((owner_grid[:, :, None] == owner_grid[:, None, :]) & earlier[None], axis=2)
    column = (jnp.arange(sources, dtype=jnp.int32)[:, None] * groups + position).reshape(-1)
    slot_count = sources * groups
    my_owners = lax.dynamic_index_in_dim(owner_grid, my_index, 0, keepdims=False)
    my_position = lax.dynamic_index_in_dim(position, my_index, 0, keepdims=False)
    target = my_owners * groups + my_position
    sender = (jnp.arange(slot_count)[:, None] == target[None, :]).astype(jnp.bfloat16)
    arrive = (slot_of[None, :] == my_index * per_owner_rows + request_ids[:, None]).astype(
        jnp.bfloat16
    )
    places = (column[:, None] == jnp.arange(slot_count)[None, :]).astype(jnp.bfloat16)
    receiver = jnp.dot(arrive, places, preferred_element_type=jnp.float32).astype(jnp.bfloat16)
    return (sender, receiver)


def ancestry(tree_links, tokens):
    parent_link = (
        tree_links[:, :, None] == jnp.arange(tokens, dtype=jnp.int32)[None, None, :]
    ).astype(jnp.float32)
    reachable = jnp.maximum(parent_link, jnp.eye(tokens, dtype=jnp.float32)[None])
    for squaring in range(max(tokens - 1, 1).bit_length()):
        reachable = jnp.minimum(
            jnp.einsum("rij,rjk->rik", reachable, reachable, precision=HIGH), 1.0
        )
    return reachable > 0.5


def cache_scores(query_rows, cache_block, cache_len, score_scale, head_size):
    key_rows = cache_block[..., :head_size].astype(jnp.float32)
    scores = jnp.einsum("rtkgd,rckd->rkgtc", query_rows, key_rows, precision=HIGH) * score_scale
    row_ids = jnp.arange(cache_block.shape[1])
    live_rows = row_ids[None, :] < cache_len[:, None]
    return jnp.where(live_rows[:, None, None, None, :], scores, -jnp.inf)


def weighted(weights, cache_block, head_size):
    return jnp.einsum(
        "rkgtc,rckd->rtkgd",
        weights,
        cache_block[..., head_size:],
        preferred_element_type=jnp.float32,
    )


def per_device(
    drafts,
    slot_of,
    lengths,
    parents,
    accepted_tokens,
    cached_key_value,
    attn_gain,
    query_weight,
    key_value_weight,
    w_out,
    mlp_gain,
    w_gate,
    w_up,
    w_down,
):
    req_count = lax.axis_size("req")
    my_index = lax.axis_index("req")
    part_index = lax.axis_index("mlp")
    per_owner_rows, tokens, quarter = drafts.shape
    sends = max(1, per_owner_rows // req_count)
    sender, receiver = route_tables(slot_of, per_owner_rows, req_count, sends, my_index)
    flat_rows = drafts.reshape(per_owner_rows, tokens * quarter)
    outgoing = jnp.dot(sender, flat_rows, preferred_element_type=jnp.float32).astype(jnp.bfloat16)
    outgoing = outgoing.reshape(req_count, sends, tokens * quarter)
    incoming = lax.all_to_all(outgoing, "req", split_axis=0, concat_axis=0, tiled=True)
    local_rows = jnp.dot(
        receiver,
        incoming.reshape(req_count * sends, tokens * quarter),
        preferred_element_type=jnp.float32,
    ).astype(jnp.bfloat16)
    local_rows = local_rows.reshape(per_owner_rows * tokens, quarter)
    full_rows = lax.all_gather(local_rows, "mlp", axis=1, tiled=True)
    wide_rows = full_rows.astype(jnp.float32)
    normalized_rows = (
        wide_rows
        * lax.rsqrt(jnp.mean(wide_rows * wide_rows, axis=1, keepdims=True) + EPS)
        * attn_gain
    ).astype(jnp.bfloat16)
    kv_heads = key_value_weight.shape[1] // (2 * HEAD_DIM)
    group_heads = query_weight.shape[1] // (kv_heads * HEAD_DIM)
    query_rows = jnp.dot(normalized_rows, query_weight, preferred_element_type=jnp.float32).reshape(
        per_owner_rows, tokens, kv_heads, group_heads, HEAD_DIM
    )
    new_key_value = (
        jnp.dot(normalized_rows, key_value_weight, preferred_element_type=jnp.float32)
        .astype(jnp.bfloat16)
        .reshape(per_owner_rows, tokens, kv_heads, 2 * HEAD_DIM)
    )
    picker = (
        accepted_tokens[:, :, None] == jnp.arange(tokens, dtype=jnp.int32)[None, None, :]
    ).astype(jnp.bfloat16)
    accepted_rows = jnp.einsum(
        "rat,rtkd->rakd", picker, new_key_value, preferred_element_type=jnp.float32
    ).astype(jnp.bfloat16)
    score_scale = 1.0 / math.sqrt(HEAD_DIM)
    draft_keys = new_key_value[..., :HEAD_DIM].astype(jnp.float32)
    draft_scores = (
        jnp.einsum("rtkgd,rjkd->rkgtj", query_rows, draft_keys, precision=HIGH) * score_scale
    )
    draft_scores = jnp.where(ancestry(parents, tokens)[:, None, None], draft_scores, -jnp.inf)
    draft_top = jnp.max(draft_scores, axis=-1)
    scores = cache_scores(query_rows, cached_key_value, lengths, score_scale, HEAD_DIM)
    row_top = jnp.maximum(draft_top, jnp.max(scores, axis=-1))
    weights = jnp.exp(scores - row_top[..., None]).astype(jnp.bfloat16)
    numerator = weighted(weights, cached_key_value, HEAD_DIM)
    denominator = jnp.sum(weights.astype(jnp.float32), axis=-1)
    draft_weights = jnp.exp(draft_scores - row_top[..., None]).astype(jnp.bfloat16)
    numerator = numerator + jnp.einsum(
        "rkgtj,rjkd->rtkgd",
        draft_weights,
        new_key_value[..., HEAD_DIM:],
        preferred_element_type=jnp.float32,
    )
    denominator = denominator + jnp.sum(draft_weights.astype(jnp.float32), axis=-1)
    attended = (numerator / jnp.transpose(denominator, (0, 3, 1, 2))[..., None]).astype(
        jnp.bfloat16
    )
    attended = attended.reshape(per_owner_rows * tokens, kv_heads * group_heads * HEAD_DIM)
    head_part = jnp.dot(attended, w_out, preferred_element_type=jnp.float32)
    attn_sum = lax.psum(head_part.astype(jnp.bfloat16), "mlp").astype(jnp.float32)
    residual = wide_rows + attn_sum
    normed_two = (
        residual * lax.rsqrt(jnp.mean(residual * residual, axis=1, keepdims=True) + EPS) * mlp_gain
    ).astype(jnp.bfloat16)
    gate_out = jnp.dot(normed_two, w_gate, preferred_element_type=jnp.float32)
    up_out = jnp.dot(normed_two, w_up, preferred_element_type=jnp.float32)
    residual_share = lax.dynamic_slice_in_dim(residual, part_index * quarter, quarter, 1)
    hidden = (jax.nn.silu(gate_out) * up_out).astype(jnp.bfloat16)
    unit_part = jnp.dot(hidden, w_down, preferred_element_type=jnp.float32)
    unit_share = lax.psum_scatter(
        unit_part.astype(jnp.bfloat16), "mlp", scatter_dimension=1, tiled=True
    ).astype(jnp.float32)
    result = (residual_share + unit_share).astype(jnp.bfloat16)
    result_rows = result.reshape(per_owner_rows, tokens * quarter)
    returning = jnp.dot(receiver.T, result_rows, preferred_element_type=jnp.float32).astype(
        jnp.bfloat16
    )
    returning = returning.reshape(req_count, sends, tokens * quarter)
    arrived = lax.all_to_all(returning, "req", split_axis=0, concat_axis=0, tiled=True)
    back_rows = jnp.dot(
        sender.T,
        arrived.reshape(req_count * sends, tokens * quarter),
        preferred_element_type=jnp.float32,
    ).astype(jnp.bfloat16)
    return (back_rows.reshape(per_owner_rows, tokens, quarter), accepted_rows)


BF = jnp.bfloat16
F32 = jnp.float32
MESH = pl.DeviceIdType.MESH
LAST = (((1,), (1,)), ((), ()))


def layer_kernel(
    slot_hbm,
    lengths_hbm,
    parents_hbm,
    accepted_hbm,
    attn_gain_hbm,
    mlp_gain_hbm,
    drafts_hbm,
    cache_hbm,
    query_hbm,
    kv_hbm,
    out_hbm,
    gate_hbm,
    up_hbm,
    down_hbm,
    layer_ref,
    accepted_ref,
    slot_of,
    lengths,
    parents,
    accepted,
    attn_gain,
    mlp_gain,
    drafts,
    cache,
    query_w,
    kv_w,
    out_w,
    gate_w,
    up_w,
    down_w,
    routed,
    gathered,
    fresh,
    attended,
    rows_one,
    one_in,
    one_out,
    one_far,
    rows_two,
    parts,
    pair_in,
    pair_out,
    far_in,
    back,
    arrived,
    load_sem,
    route_s,
    route_r,
    core_s,
    core_r,
    far_s,
    far_r,
    pass_s,
    pass_r,
    pair_s,
    pair_r,
    cross_s,
    cross_r,
    one_s,
    one_r,
    over_s,
    over_r,
    two_s,
    two_r,
    back_s,
    back_r,
):
    count = lax.axis_size("req")
    groups = lax.axis_size("mlp")
    me = lax.axis_index("req")
    part = lax.axis_index("mlp")
    near, far, diagonal = part ^ 1, part ^ 2, part ^ 3
    tokens, quarter = drafts.shape[1], drafts.shape[2]
    per = drafts.shape[0]
    total = per * tokens

    loads = [
        pltpu.make_async_copy(src, dst, load_sem.at[i])
        for i, (src, dst) in enumerate(
            (
                (drafts_hbm, drafts),
                (query_hbm, query_w),
                (kv_hbm, kv_w),
                (cache_hbm, cache),
                (out_hbm, out_w),
                (gate_hbm, gate_w),
                (up_hbm, up_w),
                (down_hbm, down_w),
                (slot_hbm, slot_of),
                (lengths_hbm, lengths),
                (parents_hbm, parents),
                (accepted_hbm, accepted),
                (attn_gain_hbm, attn_gain),
                (mlp_gain_hbm, mlp_gain),
            )
        )
    ]
    for i in (8, 0, 9, 10, 11, 12, 13, 1, 2, 3, 4, 5, 6, 7):
        loads[i].start()

    barrier = pltpu.get_barrier_semaphore()
    for d in range(1, count):
        pl.semaphore_signal(barrier, inc=1, device_id=(me ^ d, part), device_id_type=MESH)
    for d in range(1, groups):
        pl.semaphore_signal(barrier, inc=1, device_id=(me, part ^ d), device_id_type=MESH)

    loads[8].wait()
    owners = [slot_of[me * per + b] // per for b in range(per)]
    home = []
    for k in range(count):
        slot = jnp.int32(0)
        for b in range(per):
            s = slot_of[k * per + b]
            slot = jnp.where(s // per == me, s % per, slot)
        home.append(slot)

    loads[0].wait()
    for d in range(count):
        owner = me ^ d
        pick = jnp.int32(0)
        for b in range(per):
            pick = jnp.where(owners[b] == owner, b, pick)
        if d:
            routed[d] = drafts[pick]
        else:
            gathered[part, me] = drafts[pick]

    pl.semaphore_wait(barrier, count + groups - 2)

    routes = []
    for d in range(1, count):
        copy = pltpu.make_async_remote_copy(
            src_ref=routed.at[d],
            dst_ref=gathered.at[part, me],
            send_sem=route_s.at[d],
            recv_sem=route_r.at[d],
            device_id=(me ^ d, part),
            device_id_type=MESH,
        )
        copy.start()
        routes.append(copy)

    def spread(q, k, sends, recvs, d, target):
        return pltpu.make_async_remote_copy(
            src_ref=gathered.at[q, k],
            dst_ref=gathered.at[q, k],
            send_sem=sends.at[d],
            recv_sem=recvs.at[d],
            device_id=(me, target),
            device_id_type=MESH,
        )

    pending = list(routes)
    own = []
    for d in range(count):
        k = me ^ d
        if d:
            routes[d - 1].wait_recv()
        across = spread(part, k, far_s, far_r, d, far)
        across.start()
        beside = spread(part, k, core_s, core_r, d, near)
        beside.start()
        own.append((across, beside))
        pending += [across, beside]
    passed = []
    for d in range(count):
        k = me ^ d
        own[d][0].wait_recv()
        copy = spread(far, k, pass_s, pass_r, d, near)
        copy.start()
        passed.append(copy)
        pending.append(copy)

    for i in (9, 10, 11, 12, 13):
        loads[i].wait()
    link = lax.broadcasted_iota(jnp.int32, (total, per), 0) // tokens
    lane = lax.broadcasted_iota(jnp.int32, (total, per), 1)
    slot_col = jnp.zeros((total, per), jnp.int32)
    for k in range(count):
        slot_col = jnp.where(link == k, home[k], slot_col)
    expand = (slot_col == lane).astype(BF)
    tree = jnp.dot(expand, parents[...].astype(F32).astype(BF), preferred_element_type=F32)
    row_t = lax.broadcasted_iota(jnp.int32, (total, tokens), 0) % tokens
    col_t = lax.broadcasted_iota(jnp.int32, (total, tokens), 1)
    parent = jnp.sum(jnp.where(row_t == col_t, tree, 0.0), axis=1, keepdims=True)
    row_i = lax.broadcasted_iota(jnp.int32, (total, total), 0)
    col_i = lax.broadcasted_iota(jnp.int32, (total, total), 1)
    target = parent.astype(jnp.int32) + (row_i // tokens) * tokens
    reach = jnp.where((col_i == target) | (row_i == col_i), 1.0, 0.0).astype(BF)
    for _ in range(max(tokens - 1, 1).bit_length()):
        reach = jnp.minimum(jnp.dot(reach, reach, preferred_element_type=F32), 1.0).astype(BF)
    visible = reach.astype(F32) > 0.5

    length_a = accepted.shape[1]
    rows_a = per * length_a
    slot_a = lax.broadcasted_iota(jnp.int32, (rows_a, per), 0) // length_a
    expand_a = (slot_a == lax.broadcasted_iota(jnp.int32, (rows_a, per), 1)).astype(BF)
    chosen = jnp.dot(expand_a, accepted[...].astype(F32).astype(BF), preferred_element_type=F32)
    pick_a = lax.broadcasted_iota(jnp.int32, (rows_a, length_a), 0) % length_a
    col_a = lax.broadcasted_iota(jnp.int32, (rows_a, length_a), 1)
    token = jnp.sum(jnp.where(pick_a == col_a, chosen, 0.0), axis=1, keepdims=True)
    row_s = lax.broadcasted_iota(jnp.int32, (rows_a, total), 0) // length_a
    base = jnp.zeros((rows_a, total), jnp.int32)
    for k in range(count):
        base = jnp.where(row_s == home[k], k * tokens, base)
    picker = (
        lax.broadcasted_iota(jnp.int32, (rows_a, total), 1) == base + token.astype(jnp.int32)
    ).astype(BF)

    for d in range(count):
        own[d][1].wait_recv()
    for d in range(count):
        passed[d].wait_recv()

    columns = [slice(q * quarter, (q + 1) * quarter) for q in range(groups)]
    wide = [gathered[q].reshape(total, quarter).astype(F32) for q in range(groups)]
    square = sum(jnp.sum(w * w, axis=1, keepdims=True) for w in wide)
    scale = lax.rsqrt(square / (groups * quarter) + EPS)
    normed = jnp.concatenate(
        [(w * scale * attn_gain[:, c]).astype(BF) for w, c in zip(wide, columns)], axis=1
    )
    loads[1].wait()
    loads[2].wait()
    query = lax.dot_general(normed, query_w[...], LAST, preferred_element_type=F32)
    query = query * (1.0 / math.sqrt(HEAD_DIM))
    fresh[...] = jnp.dot(normed, kv_w[...], preferred_element_type=F32).astype(BF)
    fresh_kv = fresh[...]
    accepted_ref[...] = jnp.dot(picker, fresh_kv, preferred_element_type=F32).astype(BF)

    width = 2 * HEAD_DIM
    low = lax.broadcasted_iota(jnp.int32, (total, width), 1) < HEAD_DIM
    first = query[:, :width]
    third = jnp.concatenate([query[:, width:], jnp.zeros((total, HEAD_DIM), F32)], axis=1)
    heads = [
        jnp.where(low, first, 0.0),
        jnp.where(low, pltpu.roll(first, HEAD_DIM, 1), 0.0),
        third,
    ]
    loads[3].wait()
    positions = cache.shape[1]
    col_c = lax.broadcasted_iota(jnp.int32, (len(heads) * tokens, positions), 1)
    low_t = lax.broadcasted_iota(jnp.int32, (tokens, width), 1) < HEAD_DIM
    for k in range(count):
        rows = slice(k * tokens, (k + 1) * tokens)
        q = jnp.concatenate([h[rows] for h in heads], axis=0)
        high = q.astype(BF)
        rest = q - high.astype(F32)
        mid = rest.astype(BF)
        last = (rest - mid.astype(F32)).astype(BF)
        stack = jnp.concatenate([high, mid, last], axis=0)
        held = cache[home[k]]
        n = q.shape[0]
        cached = lax.dot_general(stack, held, LAST, preferred_element_type=F32)
        cached = cached[:n] + cached[n : 2 * n] + cached[2 * n :]
        draft = lax.dot_general(stack, fresh_kv, LAST, preferred_element_type=F32)
        draft = draft[:n] + draft[n : 2 * n] + draft[2 * n :]
        cached = jnp.where(col_c < lengths[home[k]], cached, -jnp.inf)
        seen = visible[rows]
        draft = jnp.where(jnp.concatenate([seen] * len(heads), axis=0), draft, -jnp.inf)
        top = jnp.maximum(
            jnp.max(cached, axis=1, keepdims=True), jnp.max(draft, axis=1, keepdims=True)
        )
        weight_c = jnp.exp(cached - top).astype(BF)
        weight_d = jnp.exp(draft - top).astype(BF)
        bottom = jnp.sum(weight_c.astype(F32), axis=1, keepdims=True) + jnp.sum(
            weight_d.astype(F32), axis=1, keepdims=True
        )
        upper = jnp.dot(weight_c, held, preferred_element_type=F32) + jnp.dot(
            weight_d, fresh_kv, preferred_element_type=F32
        )
        result = upper / bottom
        a, b, c = (result[g * tokens : (g + 1) * tokens] for g in range(3))
        attended[rows, :width] = jnp.where(low_t, pltpu.roll(a, HEAD_DIM, 1), b).astype(BF)
        attended[rows, width:] = pltpu.roll(c, HEAD_DIM, 1)[:, :HEAD_DIM].astype(BF)

    loads[4].wait()
    chunks = parts.shape[0]
    step = total // chunks

    def send(src, dst, sends, recvs, to):
        copy = pltpu.make_async_remote_copy(
            src_ref=src,
            dst_ref=dst,
            send_sem=sends,
            recv_sem=recvs,
            device_id=(me, to),
            device_id_type=MESH,
        )
        copy.start()
        pending.append(copy)
        return copy

    heads_all = attended[...]
    ahead, after, over = [], [], []
    for c in range(groups):
        product = jnp.dot(heads_all, out_w[:, columns[c]], preferred_element_type=F32)
        rows_one[c] = product.astype(BF).reshape(groups, step, quarter)
        for i, piece, out in ((0, diagonal, ahead), (1, near, after)):
            out.append(
                send(
                    rows_one.at[c, piece],
                    one_in.at[c, i],
                    one_s.at[c, i],
                    one_r.at[c, i],
                    near,
                )
            )
    for c in range(groups):
        ahead[c].wait_recv()
        one_out[c] = (rows_one[c, far].astype(F32) + one_in[c, 0].astype(F32)).astype(BF)
        over.append(send(one_out.at[c], one_far.at[c], over_s.at[c], over_r.at[c], far))
    attn, residual = [], []
    mine_rows = count // groups
    for c in range(groups):
        after[c].wait_recv()
        term = rows_one[c, part].astype(F32) + one_in[c, 1].astype(F32)
        over[c].wait_recv()
        attn.append(term + one_far[c].astype(F32))
        owned = gathered[c, pl.ds(part * mine_rows, mine_rows)].reshape(step, quarter)
        residual.append(owned.astype(F32) + attn[c])
    square = sum(jnp.sum(r * r, axis=1, keepdims=True) for r in residual)
    scale = lax.rsqrt(square / (groups * quarter) + EPS)
    shared = []
    for c in range(groups):
        rows_two[c, part] = (residual[c] * scale * mlp_gain[:, columns[c]]).astype(BF)
        mine = rows_two.at[c, part]
        shared.append(
            (
                send(mine, mine, two_s.at[0, c], two_r.at[0, c], far),
                send(mine, mine, two_s.at[1, c], two_r.at[1, c], near),
            )
        )
    relayed = []
    for c in range(groups):
        shared[c][0].wait_recv()
        other = rows_two.at[c, far]
        relayed.append(send(other, other, two_s.at[2, c], two_r.at[2, c], near))
    for c in range(groups):
        shared[c][1].wait_recv()
        relayed[c].wait_recv()
    normed_two = jnp.concatenate(
        [rows_two[c].reshape(total, quarter) for c in range(groups)], axis=1
    )
    loads[5].wait()
    loads[6].wait()
    loads[7].wait()
    gate = jnp.dot(normed_two, gate_w[...], preferred_element_type=F32)
    up = jnp.dot(normed_two, up_w[...], preferred_element_type=F32)
    hidden = (gate / (1.0 + jnp.exp(-gate)) * up).astype(BF)

    each = count // chunks
    product = jnp.dot(hidden, down_w[...], preferred_element_type=F32)
    for q in range(groups):
        for c in range(chunks):
            term = product[c * step : (c + 1) * step, columns[q]]
            parts[c, q] = (term + jnp.where(part == c, attn[q], 0.0)).astype(BF)

    def pair(c, i, piece):
        copy = pltpu.make_async_remote_copy(
            src_ref=parts.at[c, piece],
            dst_ref=pair_in.at[c, i],
            send_sem=pair_s.at[c, i],
            recv_sem=pair_r.at[c, i],
            device_id=(me, near),
            device_id_type=MESH,
        )
        copy.start()
        pending.append(copy)
        return copy

    pairs = [pair(c, 0, diagonal) for c in range(chunks)]
    mines = [pair(c, 1, near) for c in range(chunks)]
    crossed = []
    for c in range(chunks):
        pairs[c].wait_recv()
        pair_out[c] = (parts[c, far].astype(F32) + pair_in[c, 0].astype(F32)).astype(BF)
        copy = pltpu.make_async_remote_copy(
            src_ref=pair_out.at[c],
            dst_ref=far_in.at[c],
            send_sem=cross_s.at[c],
            recv_sem=cross_r.at[c],
            device_id=(me, far),
            device_id_type=MESH,
        )
        copy.start()
        crossed.append(copy)
    pending += crossed

    def give(k):
        return pltpu.make_async_remote_copy(
            src_ref=back.at[k],
            dst_ref=arrived.at[me],
            send_sem=back_s.at[k],
            recv_sem=back_r.at[me],
            device_id=(k, part),
            device_id_type=MESH,
        )

    for c in range(chunks):
        mines[c].wait_recv()
        owned = gathered[part, c * each : (c + 1) * each].reshape(step, quarter)
        mine = owned.astype(F32) + parts[c, part].astype(F32)
        mine = mine + pair_in[c, 1].astype(F32)
        crossed[c].wait_recv()
        outcome = (mine + far_in[c].astype(F32)).astype(BF)
        for j in range(each):
            k = c * each + j
            back[k] = outcome[j * tokens : (j + 1) * tokens]

            @pl.when(me != k)
            def _(k=k):
                give(k).start()

            @pl.when(me == k)
            def _(k=k):
                arrived[k] = back[k]

    def taken(o):
        return pltpu.make_async_remote_copy(
            src_ref=back.at[0],
            dst_ref=arrived.at[o],
            send_sem=back_s.at[0],
            recv_sem=back_r.at[o],
            device_id=(me, near),
            device_id_type=MESH,
        )

    for d in range(1, count):
        taken(me ^ d).wait_recv()

    for b in range(per):
        layer_ref[b] = arrived[owners[b]]

    for copy in pending:
        copy.wait_send()
    for k in range(count):

        @pl.when(me != k)
        def _(k=k):
            give(k).wait_send()


def hand_out(out_from, taken_from, out_to, taken_to, sems):
    copies = [
        pltpu.make_async_copy(out_from, out_to, sems.at[0]),
        pltpu.make_async_copy(taken_from, taken_to, sems.at[1]),
    ]
    for copy in copies:
        copy.start()
    for copy in copies:
        copy.wait()


def fused(
    drafts,
    slot_of,
    lengths,
    parents,
    accepted_tokens,
    cached_key_value,
    attn_gain,
    query_weight,
    key_value_weight,
    w_out,
    mlp_gain,
    w_gate,
    w_up,
    w_down,
):
    count = lax.axis_size("req")
    groups = lax.axis_size("mlp")
    per, tokens, quarter = drafts.shape
    accept = accepted_tokens.shape[1]
    positions, width = cached_key_value.shape[1], cached_key_value.shape[3]
    model = groups * quarter
    chunks = 4
    step = per * tokens // chunks
    total = per * tokens
    span = query_weight.shape[1]
    units = w_gate.shape[1]
    vmem = pl.BlockSpec(memory_space=pltpu.VMEM)
    hbm = pl.BlockSpec(memory_space=pltpu.HBM)
    dma = pltpu.SemaphoreType.DMA
    out, taken = pl.pallas_call(
        layer_kernel,
        out_shape=(
            jax.ShapeDtypeStruct((per, tokens, quarter), BF),
            jax.ShapeDtypeStruct((per * accept, width), BF),
        ),
        in_specs=[hbm] * 14,
        out_specs=(vmem, vmem),
        scratch_shapes=[
            pltpu.SMEM(slot_of.shape, jnp.int32),
            pltpu.SMEM(lengths.shape, jnp.int32),
            pltpu.VMEM(parents.shape, jnp.int32),
            pltpu.VMEM(accepted_tokens.shape, jnp.int32),
            pltpu.VMEM((1, model), F32),
            pltpu.VMEM((1, model), F32),
            pltpu.VMEM((per, tokens, quarter), BF),
            pltpu.VMEM((per, positions, width), BF),
            pltpu.VMEM((span, model), BF),
            pltpu.VMEM((model, width), BF),
            pltpu.VMEM((span, model), BF),
            pltpu.VMEM((model, units), BF),
            pltpu.VMEM((model, units), BF),
            pltpu.VMEM((units, model), BF),
            pltpu.VMEM((count, tokens, quarter), BF),
            pltpu.VMEM((groups, count, tokens, quarter), BF),
            pltpu.VMEM((total, width), BF),
            pltpu.VMEM((total, span), BF),
            pltpu.VMEM((groups, groups, step, quarter), BF),
            pltpu.VMEM((groups, 2, step, quarter), BF),
            pltpu.VMEM((groups, step, quarter), BF),
            pltpu.VMEM((groups, step, quarter), BF),
            pltpu.VMEM((groups, groups, step, quarter), BF),
            pltpu.VMEM((chunks, groups, step, quarter), BF),
            pltpu.VMEM((chunks, 2, step, quarter), BF),
            pltpu.VMEM((chunks, step, quarter), BF),
            pltpu.VMEM((chunks, step, quarter), BF),
            pltpu.VMEM((count, tokens, quarter), BF),
            pltpu.VMEM((count, tokens, quarter), BF),
            dma((14,)),
            dma((count,)),
            dma((count,)),
            dma((count,)),
            dma((count,)),
            dma((count,)),
            dma((count,)),
            dma((count,)),
            dma((count,)),
            dma((chunks, 2)),
            dma((chunks, 2)),
            dma((chunks,)),
            dma((chunks,)),
            dma((groups, 2)),
            dma((groups, 2)),
            dma((groups,)),
            dma((groups,)),
            dma((3, groups)),
            dma((3, groups)),
            dma((count,)),
            dma((count,)),
        ],
        compiler_params=pltpu.CompilerParams(
            collective_id=0, has_side_effects=True, vmem_limit_bytes=60 * 1024 * 1024
        ),
    )(
        slot_of,
        lengths,
        parents,
        accepted_tokens,
        attn_gain.reshape(1, model),
        mlp_gain.reshape(1, model),
        drafts,
        cached_key_value.reshape(per, positions, width),
        query_weight.T,
        key_value_weight,
        w_out,
        w_gate,
        w_up,
        w_down,
    )
    out, taken = pl.pallas_call(
        hand_out,
        out_shape=(
            jax.ShapeDtypeStruct(out.shape, BF),
            jax.ShapeDtypeStruct(taken.shape, BF),
        ),
        in_specs=[vmem, vmem],
        out_specs=(hbm, hbm),
        scratch_shapes=[dma((2,))],
    )(out, taken)
    return (out, taken.reshape(per, accept, 1, width))


def body(*args):
    drafts, cached_key_value = args[0], args[5]
    count, groups = lax.axis_size("req"), lax.axis_size("mlp")
    one_each = count == drafts.shape[0] == 8 and groups == 4
    three_heads = args[7].shape[1] == 3 * HEAD_DIM and cached_key_value.shape[2] == 1
    return (fused if one_each and three_heads else per_device)(*args)


def solution(mesh):
    placed = (
        P("req", None, "mlp"),
        P(),
        P("req"),
        P("req", None),
        P("req", None),
        P("req", None, "mlp", None),
        P(),
        P(None, "mlp"),
        P(None, "mlp"),
        P("mlp", None),
        P(),
        P(None, "mlp"),
        P(None, "mlp"),
        P("mlp", None),
    )
    return jax.shard_map(
        body,
        mesh=mesh,
        in_specs=placed,
        out_specs=(P("req", None, "mlp"), P("req", None, "mlp", None)),
        check_vma=False,
    )
```
